32 devices in a mesh: grp: 1, ex: 32 (over z, y, x, core).
Axes of the slice: x: 2, y: 2, z: 4, core: 2. Of those that a mesh axis runs over, the one named last changes fastest.
Arguments:
- example_inputs: bfloat16 [32, 1024, 4096], P(('grp', 'ex')), may hold values from -70 to 70, as said below
- output_grads: bfloat16 [32, 1024, 1024], P(('grp', 'ex')), may hold values from -70 to 70, as said below
- proj_in: bfloat16 [128, 4096], replicated, may hold values from -0.09375 to 0.09375
- proj_out: bfloat16 [64, 1024], replicated, may hold values from -0.1875 to 0.1875
- test_grads: bfloat16 [128, 8192], P('ex'), may hold values from -6 to 6
Outputs:
- scores: float32 [32, 128], P(('grp', 'ex'))
The draws below stay inside these ranges and needn't reach their ends.
Inputs may be any that keep to these rules, and one draw needn't show every extreme that they name: `example_inputs`: entries of the candidates' layer inputs lie within this range. `output_grads`: entries of the output gradients lie within this range.
All inputs are finite; a program needn't handle non-finite values.
Results may differ from the reference program's by a relative error of at most 0.0082.
Values may be sent and summed in bfloat16 or wider, within the bound.
No kernel may reach another device: no remote copies, remote signals or barrier semaphores. Data moves between devices by JAX's collectives and lax.ppermute only.
A program may use at most 128 MiB of HBM per device.

```python
import jax
import jax.numpy as jnp
from jax import lax

D = 4096
KVW = 1024
K_IN = 128
K_OUT = 64
TOK_EX = 1024
EXAMPLES = 32
TESTS = 128
KDIM = 8192


def scaled_field(key, shared_key, width, rising):
    noise_key, row_key, col_key = jax.random.split(key, 3)
    position = jnp.arange(EXAMPLES, dtype=jnp.float32) / max(EXAMPLES - 1, 1)
    order_idx = jax.random.permutation(jax.random.fold_in(shared_key, 7), EXAMPLES)
    shuffled = position[order_idx]
    if rising:
        heavy_share = 0.8 * shuffled + 0.2 * position
    else:
        heavy_share = 0.8 * (1.0 - shuffled) + 0.2 * (1.0 - position)
    base_scale = 3.0 * jnp.power(10.0, 1.5 * heavy_share - 1.5)
    row_scale = base_scale * jnp.exp(jax.random.uniform(row_key, (EXAMPLES,), jnp.float32, -0.2, 0.2))
    col_scale = jnp.exp(jax.random.uniform(col_key, (width,), jnp.float32, jnp.log(0.3), jnp.log(3.0)))
    noise = jnp.clip(jax.random.normal(noise_key, (EXAMPLES, TOK_EX, width), jnp.float32), -6.0, 6.0)
    values = noise * row_scale[:, None, None] * col_scale[None, None, :]
    return values.astype(jnp.bfloat16)


def draw_example_inputs(key, part):
    return scaled_field(jax.random.fold_in(key, 11), key, D, True)


def draw_output_grads(key, part):
    return scaled_field(jax.random.fold_in(key, 23), key, KVW, False)


def steps_of(stream_key, dims, cuts, low, largest):
    loudness = 1.0
    for axis_at, shards_of in cuts:
        heights = jax.random.uniform(jax.random.fold_in(jax.random.fold_in(stream_key, 6), axis_at), (shards_of,), jnp.float32, low / len(cuts), largest / len(cuts))
        loudness = loudness * jnp.repeat(jnp.exp(heights), dims[axis_at] // shards_of).reshape((-1,) + (1,) * (len(dims) - 1 - axis_at))
    return loudness


def bell_draw(key, dims, deviation, most, pieces=(), kind=jnp.bfloat16):
    result = jax.random.normal(key, dims, jnp.float32) * deviation
    if len(pieces) > 0:
        result = steps_of(key, dims, pieces, -0.22, 0.18) * result
    return jnp.clip(result, min=-most, max=most).astype(kind)


def setup_inputs(seed: int = 0, part: int = 0) -> dict:
    key_list = jax.random.split(jax.random.key(seed), 6)
    part_keys = jax.random.split(jax.random.fold_in(key_list[5], part), 6)
    example_inputs = draw_example_inputs(jax.random.fold_in(jax.random.fold_in(key_list[5], part), 71), part)
    output_grads = draw_output_grads(jax.random.fold_in(jax.random.fold_in(key_list[5], part), 71), part)
    proj_in = bell_draw(key_list[2], (K_IN, D), D ** -0.5, 0.09375)
    proj_out = bell_draw(key_list[3], (K_OUT, KVW), KVW ** -0.5, 0.1875)
    test_grads = bell_draw(key_list[4], (TESTS, KDIM), 1.0, 6.0, ((0, 32),))
    return {"example_inputs": example_inputs, "output_grads": output_grads, "proj_in": proj_in, "proj_out": proj_out, "test_grads": test_grads}


def damped_inverse(cov, width):
    identity = jnp.eye(width, dtype=jnp.float32)
    damped = cov + 0.1 * jnp.trace(cov) / width * identity
    factor = jnp.linalg.cholesky(damped)
    lower_inv = lax.linalg.triangular_solve(factor, identity, left_side=True, lower=True)
    return jnp.dot(lower_inv.T, lower_inv, precision=lax.Precision.HIGHEST)

def reference(example_inputs, output_grads, proj_in, proj_out, test_grads):

    def project_one(example_pair):
        inputs_one, grads_one = example_pair
        feat = jnp.dot(inputs_one.astype(jnp.float32), proj_in.T.astype(jnp.float32), preferred_element_type=jnp.float32).astype(jnp.bfloat16)
        back = jnp.dot(grads_one.astype(jnp.float32), proj_out.T.astype(jnp.float32), preferred_element_type=jnp.float32).astype(jnp.bfloat16)
        return (feat, back)
    feat_proj, grad_proj = lax.map(project_one, (example_inputs, output_grads))
    feat32 = feat_proj.astype(jnp.float32)
    grad32 = grad_proj.astype(jnp.float32)
    grads = jnp.einsum('eto,eti->eoi', grad32, feat32, precision=lax.Precision.HIGHEST)
    total_tokens = EXAMPLES * TOK_EX
    flat_feat = feat32.reshape(-1, K_IN)
    flat_grad = grad32.reshape(-1, K_OUT)
    cov_in = jnp.dot(flat_feat.T, flat_feat, precision=lax.Precision.HIGHEST) / total_tokens
    cov_out = jnp.dot(flat_grad.T, flat_grad, precision=lax.Precision.HIGHEST) / total_tokens
    inverse_in = damped_inverse(cov_in, K_IN)
    inverse_out = damped_inverse(cov_out, K_OUT)
    left = jnp.einsum('oa,eai->eoi', inverse_out, grads, precision=lax.Precision.HIGHEST)
    both = jnp.einsum('eoa,ai->eoi', left, inverse_in, precision=lax.Precision.HIGHEST)
    precond = both.reshape(EXAMPLES, K_OUT * K_IN).astype(jnp.bfloat16)
    scale = 4.0 / (K_IN * K_OUT * TOK_EX) ** 0.5
    return jnp.dot(precond.astype(jnp.float32), test_grads.T.astype(jnp.float32), preferred_element_type=jnp.float32) * scale
```

```python
import jax
import jax.numpy as jnp
from jax import lax
from jax.sharding import PartitionSpec as P

K_IN = 128
K_OUT = 64
TOK_EX = 1024


def damped_inverse(cov, width):
    identity = jnp.eye(width, dtype=jnp.float32)
    damped = cov + 0.1 * jnp.trace(cov) / width * identity
    factor = jnp.linalg.cholesky(damped)
    lower_inv = lax.linalg.triangular_solve(factor, identity, left_side=True, lower=True)
    return jnp.dot(lower_inv.T, lower_inv, precision=lax.Precision.HIGHEST)


def exchange(x, bit, devices):
    return lax.ppermute(x, "ex", [(i, i ^ bit) for i in range(devices)])


def sum_over_devices(x, devices):
    bit = 1
    while bit < devices:
        x = x + exchange(x, bit, devices)
        bit *= 2
    return x


def gather_tests(tests, devices):
    bit = devices // 2
    while bit:
        tests = jnp.concatenate([tests, exchange(tests, bit, devices)], axis=0)
        bit //= 2
    return tests


def arrival_order(devices):
    order = [0]
    bit = devices // 2
    while bit:
        order = order + [k ^ bit for k in order]
        bit //= 2
    return order


def on_device(example_inputs, output_grads, proj_in, proj_out, test_grads):
    examples_here = example_inputs.shape[0]
    devices = lax.axis_size("ex")
    if devices & (devices - 1):
        everyone = lax.all_gather(test_grads, "ex", axis=0, tiled=True)
    else:
        everyone = gather_tests(test_grads, devices)
    feat_proj = jnp.einsum(
        "etd,kd->etk", example_inputs, proj_in, preferred_element_type=jnp.float32
    ).astype(jnp.bfloat16)
    grad_proj = jnp.einsum(
        "etv,kv->etk", output_grads, proj_out, preferred_element_type=jnp.float32
    ).astype(jnp.bfloat16)
    grads = jnp.einsum("eto,eti->eoi", grad_proj, feat_proj, preferred_element_type=jnp.float32)
    flat_feat = feat_proj.reshape(-1, K_IN)
    flat_grad = grad_proj.reshape(-1, K_OUT)
    local_in = jnp.einsum("ti,tj->ij", flat_feat, flat_feat, preferred_element_type=jnp.float32)
    local_out = jnp.einsum("ti,tj->ij", flat_grad, flat_grad, preferred_element_type=jnp.float32)
    half = K_OUT // 2
    packed = jnp.concatenate(
        [local_in, jnp.concatenate([local_out[:half], local_out[half:]], axis=1)], axis=0
    )
    if devices & (devices - 1):
        packed = lax.psum(packed, "ex")
    else:
        packed = sum_over_devices(packed, devices)
    sum_in = packed[:K_IN]
    sum_out = jnp.concatenate([packed[K_IN:, :K_OUT], packed[K_IN:, K_OUT:]], axis=0)
    total_tokens = examples_here * TOK_EX * devices
    inverse_in = damped_inverse(sum_in / total_tokens, K_IN)
    inverse_out = damped_inverse(sum_out / total_tokens, K_OUT)
    scale = 4.0 / (K_IN * K_OUT * TOK_EX) ** 0.5
    left = jnp.einsum("oa,eai->eoi", inverse_out, grads, precision=lax.Precision.HIGHEST)
    both = jnp.einsum("eoa,ai->eoi", left, inverse_in, precision=lax.Precision.HIGHEST)
    precond = both.reshape(grads.shape[0], K_OUT * K_IN).astype(jnp.bfloat16)
    score_block = lax.dot_general(
        precond, everyone, (((1,), (1,)), ((), ())), preferred_element_type=jnp.float32
    )
    if devices & (devices - 1) == 0:
        per = test_grads.shape[0]
        order = jnp.array(arrival_order(devices), jnp.int32) ^ lax.axis_index("ex")
        place = (order[:, None] * per + jnp.arange(per)[None, :]).reshape(-1)
        hot = (place[:, None] == jnp.arange(devices * per)[None, :]).astype(jnp.float32)
        score_block = jnp.dot(score_block, hot, precision=lax.Precision.HIGHEST)
    return score_block * scale


def solution(mesh):
    return jax.shard_map(
        on_device,
        mesh=mesh,
        in_specs=(
            P(("grp", "ex"), None, None),
            P(("grp", "ex"), None, None),
            P(),
            P(),
            P("ex", None),
        ),
        out_specs=P(("grp", "ex"), None),
        check_vma=False,
    )
```

```python
import functools

import jax
import jax.numpy as jnp
from jax import lax
from jax.experimental import pallas as pl
from jax.experimental.pallas import tpu as pltpu
from jax.sharding import PartitionSpec as P

HIGHEST = lax.Precision.HIGHEST
DAMP = 0.1
DEPTH = 2
VMEM = pltpu.MemorySpace.VMEM
SMEM = pltpu.MemorySpace.SMEM


def dot(a, b):
    return jnp.dot(a, b, preferred_element_type=jnp.float32)


def exact(a, b):
    return jnp.dot(a, b, precision=HIGHEST, preferred_element_type=jnp.float32)


def over_last(a, b):
    return lax.dot_general(a, b, (((1,), (1,)), ((), ())), preferred_element_type=jnp.float32)


def over_first(a, b):
    return lax.dot_general(a, b, (((0,), (0,)), ((), ())), preferred_element_type=jnp.float32)


def divisor(n, most):
    return max(d for d in range(1, most + 1) if n % d == 0)


def project_kernel(x_hbm, g_hbm, pin_hbm, pout_hbm, packed_ref, grads_ref, x, g, pin, pout, pin_t, both, sx, sg, sp):
    examples = x_hbm.shape[0]
    wide, narrow = pin.shape[0], pout.shape[0]
    chunks, rows = x.shape[:2]
    per = chunks // examples
    pin_copy = pltpu.make_async_copy(pin_hbm, pin, sp.at[0])
    pout_copy = pltpu.make_async_copy(pout_hbm, pout, sp.at[1])
    pin_copy.start()
    pout_copy.start()

    def place(i):
        return i // per, pl.ds(pl.multiple_of((i % per) * rows, rows), rows)

    def copies(i):
        return (
            pltpu.make_async_copy(x_hbm.at[place(i)], x.at[i], sx.at[i]),
            pltpu.make_async_copy(g_hbm.at[place(i)], g.at[i], sg.at[i]),
        )

    for i in range(min(DEPTH, chunks)):
        for copy in copies(i):
            copy.start()
    pin_copy.wait()
    pin_t[...] = pin[...].T
    pout_copy.wait()

    @pl.loop(0, chunks)
    def _(i):
        for copy in copies(i):
            copy.wait()

        @pl.when(i + DEPTH < chunks)
        def _():
            for copy in copies(i + DEPTH):
                copy.start()

        e, tokens = place(i)
        both[e, tokens, :wide] = dot(x[i], pin_t[...]).astype(jnp.bfloat16)
        both[e, tokens, wide:] = over_last(g[i], pout[...]).astype(jnp.bfloat16)

    for e in range(examples):
        sums = over_first(both[e], both[e])
        grads_ref[e] = sums[wide:, :wide]
        low = jnp.concatenate([sums[wide:, wide:], sums[narrow:wide, narrow:wide]], axis=1)
        if e == 0:
            packed_ref[:narrow] = sums[:narrow, :wide]
            packed_ref[narrow:] = low
        else:
            packed_ref[:narrow] += sums[:narrow, :wide]
            packed_ref[narrow:] += low


def project(x, g, pin, pout):
    examples, tokens, d = x.shape
    v = g.shape[2]
    wide, narrow = pin.shape[0], pout.shape[0]
    rows = divisor(tokens, 256)
    chunks = examples * (tokens // rows)
    return pl.pallas_call(
        project_kernel,
        out_shape=[
            jax.ShapeDtypeStruct((wide, wide), jnp.float32),
            jax.ShapeDtypeStruct((examples, narrow, wide), jnp.float32),
        ],
        in_specs=[pl.BlockSpec(memory_space=pl.ANY)] * 4,
        out_specs=[pl.BlockSpec(memory_space=VMEM)] * 2,
        scratch_shapes=[
            pltpu.VMEM((chunks, rows, d), x.dtype),
            pltpu.VMEM((chunks, rows, v), g.dtype),
            pltpu.VMEM((wide, d), pin.dtype),
            pltpu.VMEM((narrow, v), pout.dtype),
            pltpu.VMEM((d, wide), pin.dtype),
            pltpu.VMEM((examples, tokens, wide + narrow), jnp.bfloat16),
            pltpu.SemaphoreType.DMA((chunks,)),
            pltpu.SemaphoreType.DMA((chunks,)),
            pltpu.SemaphoreType.DMA((2,)),
        ],
        compiler_params=pltpu.CompilerParams(vmem_limit_bytes=60 * 2**20),
        name="project",
    )(x, g, pin, pout)


def factors(n):
    spread = n / (n + 2 * DAMP)
    result = []
    while spread > 2e-6:
        result.append(2 / (2 - spread * spread))
        spread = spread * spread / (2 - spread * spread)
    return result


def normalised(s):
    n = s.shape[0]
    eye = lax.broadcasted_iota(jnp.int32, (n, n), 0) == lax.broadcasted_iota(jnp.int32, (n, n), 1)
    diagonal = jnp.sum(jnp.where(eye, s, 0.0), axis=0, keepdims=True)
    mean = jnp.sum(diagonal, axis=1, keepdims=True) / n
    first = 2 / (n + 2 * DAMP)
    return (s / mean + jnp.where(eye, DAMP, 0.0)) * first, first / mean, eye


def precond_kernel(tokens, packed_ref, grads_ref, out_ref):
    wide = packed_ref.shape[0]
    examples, narrow, _ = grads_ref.shape
    upper = packed_ref[:narrow, :]
    lower = jnp.concatenate([upper[:, narrow:].T, packed_ref[narrow:, narrow:]], axis=1)
    yi, scale_in, _ = normalised(jnp.concatenate([upper, lower], axis=0))
    yo, scale_out, eye = normalised(packed_ref[narrow:, :narrow])
    w = grads_ref[...].reshape(examples * narrow, wide)
    xo = jnp.where(eye, 1.0, 0.0)
    wides, narrows = factors(wide), factors(narrow)
    for k in range(max(len(wides), len(narrows))):
        if k < len(wides):
            if k < len(wides) - 1:
                both = jnp.concatenate([yi, w], axis=0)
                both = wides[k] * (2 * both - exact(both, yi))
                yi, w = both[:wide], both[wide:]
            else:
                w = wides[k] * (2 * w - exact(w, yi))
        if k < len(narrows):
            if k < len(narrows) - 1:
                both = jnp.concatenate([yo, xo], axis=0)
                both = narrows[k] * (2 * both - exact(both, yo))
                yo, xo = both[:narrow], both[narrow:]
            else:
                xo = narrows[k] * (2 * xo - exact(xo, yo))
    scale = (scale_in * tokens) * (scale_out * tokens)
    for e in range(examples):
        both = exact(xo, w[e * narrow : (e + 1) * narrow]) * scale
        out_ref[e] = both.astype(jnp.bfloat16).astype(jnp.float32)


def precondition(packed, grads, tokens):
    return pl.pallas_call(
        functools.partial(precond_kernel, float(tokens)),
        out_shape=jax.ShapeDtypeStruct(grads.shape, jnp.float32),
        in_specs=[pl.BlockSpec(memory_space=VMEM)] * 2,
        out_specs=pl.BlockSpec(memory_space=VMEM),
        name="precondition",
    )(packed, grads)


def score_kernel(sources, scale, me_ref, p_ref, *refs):
    pieces, out_ref = refs[:-1], refs[-1]
    examples, narrow, wide = p_ref.shape
    tests = out_ref.shape[1]
    me = me_ref[0]
    lane = lax.broadcasted_iota(jnp.int32, (1, tests), 1)
    for e in range(examples):

        def add(o, sums):
            p = p_ref[e, pl.ds(o, 1), :]
            here = pl.ds(pl.multiple_of(o * wide, wide), wide)
            return tuple(s + t[:, here].astype(jnp.float32) * p for s, t in zip(sums, pieces))

        zeros = tuple(jnp.zeros((t.shape[0], wide), jnp.float32) for t in pieces)
        sums = lax.fori_loop(0, narrow, add, zeros, unroll=4)
        total = jnp.zeros((1, tests), jnp.float32)
        for s, offsets in zip(sums, sources):
            rows = s.shape[0]
            per = rows // len(offsets)
            row = lax.broadcasted_iota(jnp.int32, (rows, 1), 0)
            target = jnp.zeros((rows, 1), jnp.int32)
            for i, offset in enumerate(offsets):
                inside = (row >= i * per) & (row < (i + 1) * per)
                target = jnp.where(inside, (me ^ offset) * per + row - i * per, target)
            by_row = jnp.sum(s, axis=1, keepdims=True)
            total += jnp.sum(jnp.where(target == lane, by_row, 0.0), axis=0, keepdims=True)
        out_ref[pl.ds(e, 1), :] = total * scale


def score(me, precond, pieces, sources, scale):
    tests = sum(t.shape[0] for t in pieces)
    return pl.pallas_call(
        functools.partial(score_kernel, sources, scale),
        out_shape=jax.ShapeDtypeStruct((precond.shape[0], tests), jnp.float32),
        in_specs=[pl.BlockSpec(memory_space=SMEM)] + [pl.BlockSpec(memory_space=VMEM)] * (1 + len(pieces)),
        out_specs=pl.BlockSpec(memory_space=VMEM),
        compiler_params=pltpu.CompilerParams(vmem_limit_bytes=32 * 2**20),
        name="score",
    )(me, precond, *pieces)


def exchange(x, bit, devices):
    return lax.ppermute(x, "ex", [(i, i ^ bit) for i in range(devices)])


def sum_over_devices(x, devices):
    bit = 1
    while bit < devices:
        x = x + exchange(x, bit, devices)
        bit *= 2
    return x


def gather_tests(tests, devices):
    offsets = [0]
    bit = devices // 2
    while bit > 4:
        tests = jnp.concatenate([tests, exchange(tests, bit, devices)], axis=0)
        offsets = offsets + [k ^ bit for k in offsets]
        bit //= 2
    pieces = [(tests, offsets)]
    if bit == 4:
        half, rows = len(offsets) // 2, tests.shape[0] // 2
        a, a_off = exchange(tests, 2, devices), [k ^ 2 for k in offsets]
        b, b_off = exchange(tests, 4, devices), [k ^ 4 for k in offsets]
        pieces += [(a, a_off), (b, b_off)]
        if half:
            pieces.append((exchange(b[:rows], 2, devices), [k ^ 2 for k in b_off[:half]]))
            pieces.append((exchange(a[rows:], 4, devices), [k ^ 4 for k in a_off[half:]]))
        else:
            pieces.append((exchange(b, 2, devices), [k ^ 2 for k in b_off]))
        bit = 1
    while bit:
        pieces += [(exchange(t, bit, devices), [k ^ bit for k in off]) for t, off in pieces]
        bit //= 2
    return [t for t, _ in pieces], [off for _, off in pieces]


def on_device(example_inputs, output_grads, proj_in, proj_out, test_grads):
    examples, tokens, _ = example_inputs.shape
    wide, narrow = proj_in.shape[0], proj_out.shape[0]
    devices = lax.axis_size("ex")
    me = lax.axis_index("ex").astype(jnp.int32)
    packed, grads = project(example_inputs, output_grads, proj_in, proj_out)
    if devices & (devices - 1):
        packed = lax.psum(packed, "ex")
        pieces = [lax.all_gather(test_grads, "ex", axis=0, tiled=True)]
        sources = [list(range(devices))]
        me = me * 0
    else:
        packed = sum_over_devices(packed, devices)
        pieces, sources = gather_tests(test_grads, devices)
    precond = precondition(packed, grads, examples * tokens * devices)
    scale = 4.0 / (wide * narrow * tokens) ** 0.5
    return score(me[None], precond, pieces, sources, scale)


def solution(mesh):
    return jax.shard_map(
        on_device,
        mesh=mesh,
        in_specs=(
            P(("grp", "ex"), None, None),
            P(("grp", "ex"), None, None),
            P(),
            P(),
            P("ex", None),
        ),
        out_specs=P(("grp", "ex"), None),
        check_vma=False,
    )
```

```python
import functools

import jax
import jax.numpy as jnp
from jax import lax
from jax.experimental import pallas as pl
from jax.experimental.pallas import tpu as pltpu
from jax.sharding import PartitionSpec as P

HIGHEST = lax.Precision.HIGHEST
DAMP = 0.1
DEPTH = 2
VMEM = pltpu.MemorySpace.VMEM
SMEM = pltpu.MemorySpace.SMEM


def dot(a, b):
    return jnp.dot(a, b, preferred_element_type=jnp.float32)


def exact(a, b):
    return jnp.dot(a, b, precision=HIGHEST, preferred_element_type=jnp.float32)


def over_last(a, b):
    return lax.dot_general(a, b, (((1,), (1,)), ((), ())), preferred_element_type=jnp.float32)


def over_first(a, b):
    return lax.dot_general(a, b, (((0,), (0,)), ((), ())), preferred_element_type=jnp.float32)


def divisor(n, most):
    return max(d for d in range(1, most + 1) if n % d == 0)


def project_kernel(x_hbm, g_hbm, pin_hbm, pout_hbm, packed_ref, grads_ref, x, g, pin, pout, pin_t, both, sx, sg, sp):
    examples = x_hbm.shape[0]
    wide, narrow = pin.shape[0], pout.shape[0]
    chunks, rows = x.shape[:2]
    per = chunks // examples
    pin_copy = pltpu.make_async_copy(pin_hbm, pin, sp.at[0])
    pout_copy = pltpu.make_async_copy(pout_hbm, pout, sp.at[1])
    pin_copy.start()
    pout_copy.start()

    def place(i):
        return i // per, pl.ds(pl.multiple_of((i % per) * rows, rows), rows)

    def copies(i):
        return (
            pltpu.make_async_copy(x_hbm.at[place(i)], x.at[i], sx.at[i]),
            pltpu.make_async_copy(g_hbm.at[place(i)], g.at[i], sg.at[i]),
        )

    for i in range(min(DEPTH, chunks)):
        for copy in copies(i):
            copy.start()
    pin_copy.wait()
    pin_t[...] = pin[...].T
    pout_copy.wait()

    @pl.loop(0, chunks)
    def _(i):
        for copy in copies(i):
            copy.wait()

        @pl.when(i + DEPTH < chunks)
        def _():
            for copy in copies(i + DEPTH):
                copy.start()

        e, tokens = place(i)
        both[e, tokens, :wide] = dot(x[i], pin_t[...]).astype(jnp.bfloat16)
        both[e, tokens, wide:] = over_last(g[i], pout[...]).astype(jnp.bfloat16)

    for e in range(examples):
        sums = over_first(both[e], both[e])
        grads_ref[e] = sums[wide:, :wide]
        low = jnp.concatenate([sums[wide:, wide:], sums[narrow:wide, narrow:wide]], axis=1)
        if e == 0:
            packed_ref[:narrow] = sums[:narrow, :wide]
            packed_ref[narrow:] = low
        else:
            packed_ref[:narrow] += sums[:narrow, :wide]
            packed_ref[narrow:] += low


def project(x, g, pin, pout):
    examples, tokens, d = x.shape
    v = g.shape[2]
    wide, narrow = pin.shape[0], pout.shape[0]
    rows = divisor(tokens, 256)
    chunks = examples * (tokens // rows)
    return pl.pallas_call(
        project_kernel,
        out_shape=[
            pltpu.VMEM((wide, wide), jnp.float32),
            pltpu.VMEM((examples, narrow, wide), jnp.float32),
        ],
        in_specs=[pl.BlockSpec(memory_space=pl.ANY)] * 4,
        out_specs=[pl.BlockSpec(memory_space=VMEM)] * 2,
        scratch_shapes=[
            pltpu.VMEM((chunks, rows, d), x.dtype),
            pltpu.VMEM((chunks, rows, v), g.dtype),
            pltpu.VMEM((wide, d), pin.dtype),
            pltpu.VMEM((narrow, v), pout.dtype),
            pltpu.VMEM((d, wide), pin.dtype),
            pltpu.VMEM((examples, tokens, wide + narrow), jnp.bfloat16),
            pltpu.SemaphoreType.DMA((chunks,)),
            pltpu.SemaphoreType.DMA((chunks,)),
            pltpu.SemaphoreType.DMA((2,)),
        ],
        compiler_params=pltpu.CompilerParams(vmem_limit_bytes=60 * 2**20),
        name="project",
    )(x, g, pin, pout)


def factors(n):
    spread = n / (n + 2 * DAMP)
    result = []
    while spread > 2e-6:
        result.append(2 / (2 - spread * spread))
        spread = spread * spread / (2 - spread * spread)
    return result


def normalised(s):
    n = s.shape[0]
    eye = lax.broadcasted_iota(jnp.int32, (n, n), 0) == lax.broadcasted_iota(jnp.int32, (n, n), 1)
    diagonal = jnp.sum(jnp.where(eye, s, 0.0), axis=0, keepdims=True)
    mean = jnp.sum(diagonal, axis=1, keepdims=True) / n
    first = 2 / (n + 2 * DAMP)
    return (s / mean + jnp.where(eye, DAMP, 0.0)) * first, first / mean, eye


def precond_kernel(tokens, here_ref, there_ref, grads_ref, out_ref):
    wide = here_ref.shape[0]
    examples, narrow, _ = grads_ref.shape
    packed = here_ref[...] + there_ref[...]
    upper = packed[:narrow]
    lower = jnp.concatenate([upper[:, narrow:].T, packed[narrow:, narrow:]], axis=1)
    yi, scale_in, _ = normalised(jnp.concatenate([upper, lower], axis=0))
    yo, scale_out, eye = normalised(packed[narrow:, :narrow])
    w = grads_ref[...].reshape(examples * narrow, wide)
    xo = jnp.where(eye, 1.0, 0.0)
    wides, narrows = factors(wide), factors(narrow)
    for k in range(max(len(wides), len(narrows))):
        if k < len(wides):
            if k < len(wides) - 1:
                both = jnp.concatenate([yi, w], axis=0)
                both = wides[k] * (2 * both - exact(both, yi))
                yi, w = both[:wide], both[wide:]
            else:
                w = wides[k] * (2 * w - exact(w, yi))
        if k < len(narrows):
            if k < len(narrows) - 1:
                both = jnp.concatenate([yo, xo], axis=0)
                both = narrows[k] * (2 * both - exact(both, yo))
                yo, xo = both[:narrow], both[narrow:]
            else:
                xo = narrows[k] * (2 * xo - exact(xo, yo))
    scale = (scale_in * tokens) * (scale_out * tokens)
    for e in range(examples):
        both = exact(xo, w[e * narrow : (e + 1) * narrow]) * scale
        out_ref[e] = both.astype(jnp.bfloat16).astype(jnp.float32)


def precondition(here, there, grads, tokens):
    return pl.pallas_call(
        functools.partial(precond_kernel, float(tokens)),
        out_shape=pltpu.VMEM(grads.shape, jnp.float32),
        in_specs=[pl.BlockSpec(memory_space=VMEM)] * 3,
        out_specs=pl.BlockSpec(memory_space=VMEM),
        name="precondition",
    )(*[pltpu.with_memory_space_constraint(a, VMEM) for a in (here, there, grads)])


def score_kernel(sources, scale, me_ref, p_ref, *refs):
    pieces, out_ref = refs[:-1], refs[-1]
    examples, narrow, wide = p_ref.shape
    tests = out_ref.shape[1]
    me = me_ref[0]
    lane = lax.broadcasted_iota(jnp.int32, (1, tests), 1)
    for e in range(examples):

        def add(o, sums):
            p = p_ref[e, pl.ds(o, 1), :]
            here = pl.ds(pl.multiple_of(o * wide, wide), wide)
            return tuple(s + t[:, here].astype(jnp.float32) * p for s, t in zip(sums, pieces))

        zeros = tuple(jnp.zeros((t.shape[0], wide), jnp.float32) for t in pieces)
        sums = lax.fori_loop(0, narrow, add, zeros, unroll=4)
        total = jnp.zeros((1, tests), jnp.float32)
        for s, offsets in zip(sums, sources):
            rows = s.shape[0]
            per = rows // len(offsets)
            row = lax.broadcasted_iota(jnp.int32, (rows, 1), 0)
            target = jnp.zeros((rows, 1), jnp.int32)
            for i, offset in enumerate(offsets):
                inside = (row >= i * per) & (row < (i + 1) * per)
                target = jnp.where(inside, (me ^ offset) * per + row - i * per, target)
            by_row = jnp.sum(s, axis=1, keepdims=True)
            total += jnp.sum(jnp.where(target == lane, by_row, 0.0), axis=0, keepdims=True)
        out_ref[pl.ds(e, 1), :] = total * scale


def score(me, precond, pieces, sources, scale):
    tests = sum(t.shape[0] for t in pieces)
    return pl.pallas_call(
        functools.partial(score_kernel, sources, scale),
        out_shape=jax.ShapeDtypeStruct((precond.shape[0], tests), jnp.float32),
        in_specs=[pl.BlockSpec(memory_space=SMEM)] + [pl.BlockSpec(memory_space=VMEM)] * (1 + len(pieces)),
        out_specs=pl.BlockSpec(memory_space=VMEM),
        compiler_params=pltpu.CompilerParams(vmem_limit_bytes=32 * 2**20),
        name="score",
    )(me, *[pltpu.with_memory_space_constraint(a, VMEM) for a in (precond, *pieces)])


def exchange(x, bit, devices):
    return lax.ppermute(x, "ex", [(i, i ^ bit) for i in range(devices)])


def join(tests, offsets, bit, devices):
    both = jnp.concatenate([tests, exchange(tests, bit, devices)], axis=0)
    return both, offsets + [k ^ bit for k in offsets]


def exchange_all(packed, tests, tests_offsets, devices):
    far = devices // 4
    packed, tests = lax.optimization_barrier((packed, tests))
    packed = packed + exchange(packed, 1, devices)
    packed = packed + exchange(packed, 2, devices)
    offsets = tests_offsets
    while far > 4:
        tests, offsets = join(tests, offsets, far, devices)
        far //= 2
    packed, tests = lax.optimization_barrier((packed, tests))
    half, rows = len(offsets) // 2, tests.shape[0] // 2
    a, a_off = exchange(tests, 2, devices), [k ^ 2 for k in offsets]
    b, b_off = exchange(tests, 4, devices), [k ^ 4 for k in offsets]
    packed = packed + exchange(packed, 4, devices)
    packed = packed + exchange(packed, 8, devices)
    bit = 16
    while bit < devices // 2:
        packed = packed + exchange(packed, bit, devices)
        bit *= 2
    packed, a, b = lax.optimization_barrier((packed, a, b))
    pieces = [
        (tests, offsets),
        (a, a_off),
        (b, b_off),
        (exchange(b[:rows], 2, devices), [k ^ 2 for k in b_off[:half]]),
        (exchange(a[rows:], 4, devices), [k ^ 4 for k in a_off[half:]]),
    ]
    pieces += [(exchange(t, 1, devices), [k ^ 1 for k in off]) for t, off in pieces]
    there = exchange(packed, bit, devices)
    return packed, there, [t for t, _ in pieces], [off for _, off in pieces]


def on_device(example_inputs, output_grads, proj_in, proj_out, test_grads):
    examples, tokens, _ = example_inputs.shape
    wide, narrow = proj_in.shape[0], proj_out.shape[0]
    devices = lax.axis_size("ex")
    me = lax.axis_index("ex").astype(jnp.int32)
    simple = devices < 32 or devices & (devices - 1)
    if not simple:
        far = exchange(test_grads, devices // 2, devices)
    packed, grads = project(example_inputs, output_grads, proj_in, proj_out)
    if simple:
        here, there = lax.psum(packed, "ex"), jnp.zeros_like(packed)
        pieces = [lax.all_gather(test_grads, "ex", axis=0, tiled=True)]
        sources = [list(range(devices))]
        me = me * 0
    else:
        packed, far = lax.optimization_barrier((packed, far))
        tests = jnp.concatenate([test_grads, far], axis=0)
        here, there, pieces, sources = exchange_all(packed, tests, [0, devices // 2], devices)
    precond = precondition(here, there, grads, examples * tokens * devices)
    scale = 4.0 / (wide * narrow * tokens) ** 0.5
    return score(me[None], precond, pieces, sources, scale)


def solution(mesh):
    return jax.shard_map(
        on_device,
        mesh=mesh,
        in_specs=(
            P(("grp", "ex"), None, None),
            P(("grp", "ex"), None, None),
            P(),
            P(),
            P("ex", None),
        ),
        out_specs=P(("grp", "ex"), None),
        check_vma=False,
    )
```

```python
import functools

import jax
import jax.numpy as jnp
from jax import lax
from jax.experimental import pallas as pl
from jax.experimental.pallas import tpu as pltpu
from jax.sharding import PartitionSpec as P

HIGHEST = lax.Precision.HIGHEST
DAMP = 0.1
DEPTH = 2
VMEM = pltpu.MemorySpace.VMEM
SMEM = pltpu.MemorySpace.SMEM


def dot(a, b):
    return jnp.dot(a, b, preferred_element_type=jnp.float32)


def exact(a, b):
    return jnp.dot(a, b, precision=HIGHEST, preferred_element_type=jnp.float32)


def over_last(a, b):
    return lax.dot_general(a, b, (((1,), (1,)), ((), ())), preferred_element_type=jnp.float32)


def over_first(a, b):
    return lax.dot_general(a, b, (((0,), (0,)), ((), ())), preferred_element_type=jnp.float32)


def divisor(n, most):
    return max(d for d in range(1, most + 1) if n % d == 0)


def project_kernel(x_hbm, g_hbm, pin_hbm, pout_hbm, packed_ref, grads_ref, x, g, pin, pout, pin_t, both, sx, sg, sp):
    examples = x_hbm.shape[0]
    wide, narrow = pin.shape[0], pout.shape[0]
    chunks, rows = x.shape[:2]
    per = chunks // examples
    pin_copy = pltpu.make_async_copy(pin_hbm, pin, sp.at[0])
    pout_copy = pltpu.make_async_copy(pout_hbm, pout, sp.at[1])
    pin_copy.start()
    pout_copy.start()

    def place(i):
        return i // per, pl.ds(pl.multiple_of((i % per) * rows, rows), rows)

    def copies(i):
        return (
            pltpu.make_async_copy(x_hbm.at[place(i)], x.at[i], sx.at[i]),
            pltpu.make_async_copy(g_hbm.at[place(i)], g.at[i], sg.at[i]),
        )

    for i in range(min(DEPTH, chunks)):
        for copy in copies(i):
            copy.start()
    pin_copy.wait()
    pin_t[...] = pin[...].T
    pout_copy.wait()

    @pl.loop(0, chunks)
    def _(i):
        for copy in copies(i):
            copy.wait()

        @pl.when(i + DEPTH < chunks)
        def _():
            for copy in copies(i + DEPTH):
                copy.start()

        e, tokens = place(i)
        both[e, tokens, :wide] = dot(x[i], pin_t[...]).astype(jnp.bfloat16)
        both[e, tokens, wide:] = over_last(g[i], pout[...]).astype(jnp.bfloat16)

    for e in range(examples):
        sums = over_first(both[e], both[e])
        grads_ref[e] = sums[wide:, :wide]
        low = jnp.concatenate([sums[wide:, wide:], sums[narrow:wide, narrow:wide]], axis=1)
        if e == 0:
            packed_ref[:narrow] = sums[:narrow, :wide]
            packed_ref[narrow:] = low
        else:
            packed_ref[:narrow] += sums[:narrow, :wide]
            packed_ref[narrow:] += low


def project(x, g, pin, pout):
    examples, tokens, d = x.shape
    v = g.shape[2]
    wide, narrow = pin.shape[0], pout.shape[0]
    rows = divisor(tokens, 256)
    chunks = examples * (tokens // rows)
    return pl.pallas_call(
        project_kernel,
        out_shape=[
            pltpu.VMEM((wide, wide), jnp.float32),
            pltpu.VMEM((examples, narrow, wide), jnp.float32),
        ],
        in_specs=[pl.BlockSpec(memory_space=pl.ANY)] * 4,
        out_specs=[pl.BlockSpec(memory_space=VMEM)] * 2,
        scratch_shapes=[
            pltpu.VMEM((chunks, rows, d), x.dtype),
            pltpu.VMEM((chunks, rows, v), g.dtype),
            pltpu.VMEM((wide, d), pin.dtype),
            pltpu.VMEM((narrow, v), pout.dtype),
            pltpu.VMEM((d, wide), pin.dtype),
            pltpu.VMEM((examples, tokens, wide + narrow), jnp.bfloat16),
            pltpu.SemaphoreType.DMA((chunks,)),
            pltpu.SemaphoreType.DMA((chunks,)),
            pltpu.SemaphoreType.DMA((2,)),
        ],
        compiler_params=pltpu.CompilerParams(vmem_limit_bytes=60 * 2**20),
        name="project",
    )(x, g, pin, pout)


def factors(n):
    spread = n / (n + 2 * DAMP)
    result = []
    while spread > 2e-6:
        result.append(2 / (2 - spread * spread))
        spread = spread * spread / (2 - spread * spread)
    return result


def normalised(s):
    n = s.shape[0]
    eye = lax.broadcasted_iota(jnp.int32, (n, n), 0) == lax.broadcasted_iota(jnp.int32, (n, n), 1)
    diagonal = jnp.sum(jnp.where(eye, s, 0.0), axis=0, keepdims=True)
    mean = jnp.sum(diagonal, axis=1, keepdims=True) / n
    first = 2 / (n + 2 * DAMP)
    return (s / mean + jnp.where(eye, DAMP, 0.0)) * first, first / mean, eye


def precond_kernel(tokens, here_ref, there_ref, grads_ref, out_ref):
    wide = here_ref.shape[0]
    examples, narrow, _ = grads_ref.shape
    packed = here_ref[...] + there_ref[...]
    upper = packed[:narrow]
    lower = jnp.concatenate([upper[:, narrow:].T, packed[narrow:, narrow:]], axis=1)
    yi, scale_in, _ = normalised(jnp.concatenate([upper, lower], axis=0))
    yo, scale_out, eye = normalised(packed[narrow:, :narrow])
    w = grads_ref[...].reshape(examples * narrow, wide)
    xo = jnp.where(eye, 1.0, 0.0)
    wides, narrows = factors(wide), factors(narrow)
    for k in range(max(len(wides), len(narrows))):
        if k < len(wides):
            if k < len(wides) - 1:
                both = jnp.concatenate([yi, w], axis=0)
                both = wides[k] * (2 * both - exact(both, yi))
                yi, w = both[:wide], both[wide:]
            else:
                w = wides[k] * (2 * w - exact(w, yi))
        if k < len(narrows):
            if k < len(narrows) - 1:
                both = jnp.concatenate([yo, xo], axis=0)
                both = narrows[k] * (2 * both - exact(both, yo))
                yo, xo = both[:narrow], both[narrow:]
            else:
                xo = narrows[k] * (2 * xo - exact(xo, yo))
    scale = (scale_in * tokens) * (scale_out * tokens)
    for e in range(examples):
        both = exact(xo, w[e * narrow : (e + 1) * narrow]) * scale
        out_ref[e] = both.astype(jnp.bfloat16).astype(jnp.float32)


def precondition(here, there, grads, tokens):
    return pl.pallas_call(
        functools.partial(precond_kernel, float(tokens)),
        out_shape=pltpu.VMEM(grads.shape, jnp.float32),
        in_specs=[pl.BlockSpec(memory_space=VMEM)] * 3,
        out_specs=pl.BlockSpec(memory_space=VMEM),
        name="precondition",
    )(*[pltpu.with_memory_space_constraint(a, VMEM) for a in (here, there, grads)])


def score_kernel(sources, scale, me_ref, p_ref, *refs):
    pieces, out_ref = refs[:-1], refs[-1]
    examples, narrow, wide = p_ref.shape
    tests = out_ref.shape[1]
    me = me_ref[0]
    lane = lax.broadcasted_iota(jnp.int32, (1, tests), 1)
    for e in range(examples):

        def add(o, sums):
            p = p_ref[e, pl.ds(o, 1), :]
            here = pl.ds(pl.multiple_of(o * wide, wide), wide)
            return tuple(s + t[:, here].astype(jnp.float32) * p for s, t in zip(sums, pieces))

        zeros = tuple(jnp.zeros((t.shape[0], wide), jnp.float32) for t in pieces)
        sums = lax.fori_loop(0, narrow, add, zeros, unroll=4)
        total = jnp.zeros((1, tests), jnp.float32)
        for s, offsets in zip(sums, sources):
            rows = s.shape[0]
            per = rows // len(offsets)
            row = lax.broadcasted_iota(jnp.int32, (rows, 1), 0)
            target = jnp.zeros((rows, 1), jnp.int32)
            for i, offset in enumerate(offsets):
                inside = (row >= i * per) & (row < (i + 1) * per)
                target = jnp.where(inside, (me ^ offset) * per + row - i * per, target)
            by_row = jnp.sum(s, axis=1, keepdims=True)
            total += jnp.sum(jnp.where(target == lane, by_row, 0.0), axis=0, keepdims=True)
        out_ref[pl.ds(e, 1), :] = total * scale


def score(me, precond, pieces, sources, scale):
    tests = sum(t.shape[0] for t in pieces)
    return pl.pallas_call(
        functools.partial(score_kernel, sources, scale),
        out_shape=jax.ShapeDtypeStruct((precond.shape[0], tests), jnp.float32),
        in_specs=[pl.BlockSpec(memory_space=SMEM)] + [pl.BlockSpec(memory_space=VMEM)] * (1 + len(pieces)),
        out_specs=pl.BlockSpec(memory_space=VMEM),
        compiler_params=pltpu.CompilerParams(vmem_limit_bytes=32 * 2**20),
        name="score",
    )(me, *[pltpu.with_memory_space_constraint(a, VMEM) for a in (precond, *pieces)])


def exchange(x, bit, devices):
    return lax.ppermute(x, "ex", [(i, i ^ bit) for i in range(devices)])


def join(tests, offsets, bit, devices):
    both = jnp.concatenate([tests, exchange(tests, bit, devices)], axis=0)
    return both, offsets + [k ^ bit for k in offsets]


def exchange_all(packed, tests, offsets, devices):
    far = devices // 4
    packed, tests = lax.optimization_barrier((packed, tests))
    packed = packed + exchange(packed, 1, devices)
    packed = packed + exchange(packed, 2, devices)
    while far > 4:
        tests, offsets = join(tests, offsets, far, devices)
        far //= 2
    packed, tests = lax.optimization_barrier((packed, tests))
    half, rows = len(offsets) // 2, tests.shape[0] // 2
    a, a_off = exchange(tests, 2, devices), [k ^ 2 for k in offsets]
    b, b_off = exchange(tests, 4, devices), [k ^ 4 for k in offsets]
    bit = 8
    while bit < devices:
        packed = packed + exchange(packed, bit, devices)
        bit *= 2
    packed, a, b = lax.optimization_barrier((packed, a, b))
    pieces = [
        (tests, offsets),
        (a, a_off),
        (b, b_off),
        (exchange(b[:rows], 2, devices), [k ^ 2 for k in b_off[:half]]),
        (exchange(a[rows:], 4, devices), [k ^ 4 for k in a_off[half:]]),
    ]
    pieces += [(exchange(t, 1, devices), [k ^ 1 for k in off]) for t, off in pieces]
    there = exchange(packed, 4, devices)
    return packed, there, [t for t, _ in pieces], [off for _, off in pieces]


def on_device(example_inputs, output_grads, proj_in, proj_out, test_grads):
    examples, tokens, _ = example_inputs.shape
    wide, narrow = proj_in.shape[0], proj_out.shape[0]
    devices = lax.axis_size("ex")
    me = lax.axis_index("ex").astype(jnp.int32)
    simple = devices < 32 or devices & (devices - 1)
    if not simple:
        far = exchange(test_grads, devices // 2, devices)
    packed, grads = project(example_inputs, output_grads, proj_in, proj_out)
    if simple:
        here, there = lax.psum(packed, "ex"), jnp.zeros_like(packed)
        pieces = [lax.all_gather(test_grads, "ex", axis=0, tiled=True)]
        sources = [list(range(devices))]
        me = me * 0
    else:
        packed, far = lax.optimization_barrier((packed, far))
        tests = jnp.concatenate([test_grads, far], axis=0)
        here, there, pieces, sources = exchange_all(packed, tests, [0, devices // 2], devices)
    precond = precondition(here, there, grads, examples * tokens * devices)
    scale = 4.0 / (wide * narrow * tokens) ** 0.5
    return score(me[None], precond, pieces, sources, scale)


def solution(mesh):
    return jax.shard_map(
        on_device,
        mesh=mesh,
        in_specs=(
            P(("grp", "ex"), None, None),
            P(("grp", "ex"), None, None),
            P(),
            P(),
            P("ex", None),
        ),
        out_specs=P(("grp", "ex"), None),
        check_vma=False,
    )
```

```python
import functools

import jax
import jax.numpy as jnp
from jax import lax
from jax.experimental import pallas as pl
from jax.experimental.pallas import tpu as pltpu
from jax.sharding import PartitionSpec as P

HIGHEST = lax.Precision.HIGHEST
DAMP = 0.1
DEPTH = 2
LONG = 10**10
VMEM = pltpu.MemorySpace.VMEM
SMEM = pltpu.MemorySpace.SMEM


def dot(a, b):
    return jnp.dot(a, b, preferred_element_type=jnp.float32)


def exact(a, b):
    return jnp.dot(a, b, precision=HIGHEST, preferred_element_type=jnp.float32)


def over_last(a, b):
    return lax.dot_general(a, b, (((1,), (1,)), ((), ())), preferred_element_type=jnp.float32)


def over_first(a, b):
    return lax.dot_general(a, b, (((0,), (0,)), ((), ())), preferred_element_type=jnp.float32)


def divisor(n, most):
    return max(d for d in range(1, most + 1) if n % d == 0)


def project_kernel(x_hbm, g_hbm, pin_hbm, pout_hbm, packed_ref, grads_ref, x, g, pin, pout, pin_t, both, sx, sg, sp):
    examples = x_hbm.shape[0]
    wide, narrow = pin.shape[0], pout.shape[0]
    chunks, rows = x.shape[:2]
    per = chunks // examples
    pin_copy = pltpu.make_async_copy(pin_hbm, pin, sp.at[0])
    pout_copy = pltpu.make_async_copy(pout_hbm, pout, sp.at[1])
    pin_copy.start()
    pout_copy.start()

    def place(i):
        return i // per, pl.ds(pl.multiple_of((i % per) * rows, rows), rows)

    def copies(i):
        return (
            pltpu.make_async_copy(x_hbm.at[place(i)], x.at[i], sx.at[i]),
            pltpu.make_async_copy(g_hbm.at[place(i)], g.at[i], sg.at[i]),
        )

    for i in range(min(DEPTH, chunks)):
        for copy in copies(i):
            copy.start()
    pin_copy.wait()
    pin_t[...] = pin[...].T
    pout_copy.wait()

    @pl.loop(0, chunks)
    def _(i):
        for copy in copies(i):
            copy.wait()

        @pl.when(i + DEPTH < chunks)
        def _():
            for copy in copies(i + DEPTH):
                copy.start()

        e, tokens = place(i)
        both[e, tokens, :wide] = dot(x[i], pin_t[...]).astype(jnp.bfloat16)
        both[e, tokens, wide:] = over_last(g[i], pout[...]).astype(jnp.bfloat16)

    for e in range(examples):
        sums = over_first(both[e], both[e])
        grads_ref[e] = sums[wide:, :wide]
        low = jnp.concatenate([sums[wide:, wide:], sums[narrow:wide, narrow:wide]], axis=1)
        if e == 0:
            packed_ref[:narrow] = sums[:narrow, :wide]
            packed_ref[narrow:] = low
        else:
            packed_ref[:narrow] += sums[:narrow, :wide]
            packed_ref[narrow:] += low


def project(x, g, pin, pout):
    examples, tokens, d = x.shape
    v = g.shape[2]
    wide, narrow = pin.shape[0], pout.shape[0]
    rows = divisor(tokens, 256)
    chunks = examples * (tokens // rows)
    return pl.pallas_call(
        project_kernel,
        out_shape=[
            pltpu.VMEM((wide, wide), jnp.float32),
            pltpu.VMEM((examples, narrow, wide), jnp.float32),
        ],
        in_specs=[pl.BlockSpec(memory_space=pl.ANY)] * 4,
        out_specs=[pl.BlockSpec(memory_space=VMEM)] * 2,
        scratch_shapes=[
            pltpu.VMEM((chunks, rows, d), x.dtype),
            pltpu.VMEM((chunks, rows, v), g.dtype),
            pltpu.VMEM((wide, d), pin.dtype),
            pltpu.VMEM((narrow, v), pout.dtype),
            pltpu.VMEM((d, wide), pin.dtype),
            pltpu.VMEM((examples, tokens, wide + narrow), jnp.bfloat16),
            pltpu.SemaphoreType.DMA((chunks,)),
            pltpu.SemaphoreType.DMA((chunks,)),
            pltpu.SemaphoreType.DMA((2,)),
        ],
        compiler_params=pltpu.CompilerParams(vmem_limit_bytes=60 * 2**20),
        name="project",
    )(x, g, pin, pout)


def factors(n):
    spread = n / (n + 2 * DAMP)
    result = []
    while spread > 2e-6:
        result.append(2 / (2 - spread * spread))
        spread = spread * spread / (2 - spread * spread)
    return result


def normalised(s):
    n = s.shape[0]
    eye = lax.broadcasted_iota(jnp.int32, (n, n), 0) == lax.broadcasted_iota(jnp.int32, (n, n), 1)
    diagonal = jnp.sum(jnp.where(eye, s, 0.0), axis=0, keepdims=True)
    mean = jnp.sum(diagonal, axis=1, keepdims=True) / n
    first = 2 / (n + 2 * DAMP)
    return (s / mean + jnp.where(eye, DAMP, 0.0)) * first, first / mean, eye


def precond_kernel(tokens, packed_ref, grads_ref, out_ref):
    wide = packed_ref.shape[0]
    examples, narrow, _ = grads_ref.shape
    packed = packed_ref[...]
    upper = packed[:narrow]
    lower = jnp.concatenate([upper[:, narrow:].T, packed[narrow:, narrow:]], axis=1)
    yi, scale_in, _ = normalised(jnp.concatenate([upper, lower], axis=0))
    yo, scale_out, eye = normalised(packed[narrow:, :narrow])
    w = grads_ref[...].reshape(examples * narrow, wide)
    xo = jnp.where(eye, 1.0, 0.0)
    wides, narrows = factors(wide), factors(narrow)
    for k in range(max(len(wides), len(narrows))):
        if k < len(wides):
            if k < len(wides) - 1:
                both = jnp.concatenate([yi, w], axis=0)
                both = wides[k] * (2 * both - exact(both, yi))
                yi, w = both[:wide], both[wide:]
            else:
                w = wides[k] * (2 * w - exact(w, yi))
        if k < len(narrows):
            if k < len(narrows) - 1:
                both = jnp.concatenate([yo, xo], axis=0)
                both = narrows[k] * (2 * both - exact(both, yo))
                yo, xo = both[:narrow], both[narrow:]
            else:
                xo = narrows[k] * (2 * xo - exact(xo, yo))
    scale = (scale_in * tokens) * (scale_out * tokens)
    for e in range(examples):
        both = exact(xo, w[e * narrow : (e + 1) * narrow]) * scale
        out_ref[e] = both.astype(jnp.bfloat16).astype(jnp.float32)


def precondition(packed, grads, tokens):
    return pl.pallas_call(
        functools.partial(precond_kernel, float(tokens)),
        out_shape=pltpu.VMEM(grads.shape, jnp.float32),
        in_specs=[pl.BlockSpec(memory_space=VMEM)] * 2,
        out_specs=pl.BlockSpec(memory_space=VMEM),
        name="precondition",
    )(*[pltpu.with_memory_space_constraint(a, VMEM) for a in (packed, grads)])


def score_kernel(sources, scale, me_ref, p_ref, *refs):
    pieces, out_ref = refs[:-1], refs[-1]
    examples, narrow, wide = p_ref.shape
    tests = out_ref.shape[1]
    me = me_ref[0]
    lane = lax.broadcasted_iota(jnp.int32, (1, tests), 1)
    for e in range(examples):

        def add(o, sums):
            p = p_ref[e, pl.ds(o, 1), :]
            here = pl.ds(pl.multiple_of(o * wide, wide), wide)
            return tuple(s + t[:, here].astype(jnp.float32) * p for s, t in zip(sums, pieces))

        zeros = tuple(jnp.zeros((t.shape[0], wide), jnp.float32) for t in pieces)
        sums = lax.fori_loop(0, narrow, add, zeros, unroll=4)
        total = jnp.zeros((1, tests), jnp.float32)
        for s, offsets in zip(sums, sources):
            rows = s.shape[0]
            per = rows // len(offsets)
            row = lax.broadcasted_iota(jnp.int32, (rows, 1), 0)
            target = jnp.zeros((rows, 1), jnp.int32)
            for i, offset in enumerate(offsets):
                inside = (row >= i * per) & (row < (i + 1) * per)
                target = jnp.where(inside, (me ^ offset) * per + row - i * per, target)
            by_row = jnp.sum(s, axis=1, keepdims=True)
            total += jnp.sum(jnp.where(target == lane, by_row, 0.0), axis=0, keepdims=True)
        out_ref[pl.ds(e, 1), :] = total * scale


def score(me, precond, pieces, sources, scale):
    tests = sum(t.shape[0] for t in pieces)
    return pl.pallas_call(
        functools.partial(score_kernel, sources, scale),
        out_shape=jax.ShapeDtypeStruct((precond.shape[0], tests), jnp.float32),
        in_specs=[pl.BlockSpec(memory_space=SMEM)] + [pl.BlockSpec(memory_space=VMEM)] * (1 + len(pieces)),
        out_specs=pl.BlockSpec(memory_space=VMEM),
        compiler_params=pltpu.CompilerParams(vmem_limit_bytes=32 * 2**20),
        name="score",
    )(me, *[pltpu.with_memory_space_constraint(a, VMEM) for a in (precond, *pieces)])


def exchange(x, bit, devices):
    return lax.ppermute(x, "ex", [(i, i ^ bit) for i in range(devices)])


def join(tests, offsets, bit, devices):
    both = jnp.concatenate([tests, exchange(tests, bit, devices)], axis=0)
    return both, offsets + [k ^ bit for k in offsets]


def add_kernel(a_ref, b_ref, out_ref):
    out_ref[...] = a_ref[...] + b_ref[...]


def add_late(a, b):
    return pl.pallas_call(
        add_kernel,
        out_shape=pltpu.VMEM(a.shape, a.dtype),
        in_specs=[pl.BlockSpec(memory_space=VMEM)] * 2,
        out_specs=pl.BlockSpec(memory_space=VMEM),
        cost_estimate=pl.CostEstimate(flops=LONG, bytes_accessed=3 * a.size * 4, transcendentals=0),
        name="add",
    )(*[pltpu.with_memory_space_constraint(t, VMEM) for t in (a, b)])


def exchange_all(packed, tests, offsets, devices):
    far = devices // 4
    packed, tests = lax.optimization_barrier((packed, tests))
    packed = packed + exchange(packed, 1, devices)
    packed = packed + exchange(packed, 2, devices)
    while far > 4:
        tests, offsets = join(tests, offsets, far, devices)
        far //= 2
    packed, tests = lax.optimization_barrier((packed, tests))
    half, rows = len(offsets) // 2, tests.shape[0] // 2
    a, a_off = exchange(tests, 2, devices), [k ^ 2 for k in offsets]
    b, b_off = exchange(tests, 4, devices), [k ^ 4 for k in offsets]
    packed = add_late(packed, exchange(packed, 8, devices))
    bit = 16
    while bit < devices:
        packed = packed + exchange(packed, bit, devices)
        bit *= 2
    packed, a, b = lax.optimization_barrier((packed, a, b))
    c, c_off = exchange(b[:rows], 2, devices), [k ^ 2 for k in b_off[:half]]
    d, d_off = exchange(a[rows:], 4, devices), [k ^ 4 for k in a_off[half:]]
    packed = add_late(packed, exchange(packed, 4, devices))
    packed, c, d, tests, a, b = lax.optimization_barrier((packed, c, d, tests, a, b))
    everyone = jnp.concatenate([tests, a, b, c, d], axis=0)
    offsets = offsets + a_off + b_off + c_off + d_off
    pieces = [(everyone, offsets), (exchange(everyone, 1, devices), [k ^ 1 for k in offsets])]
    return packed, [t for t, _ in pieces], [off for _, off in pieces]


def on_device(example_inputs, output_grads, proj_in, proj_out, test_grads):
    examples, tokens, _ = example_inputs.shape
    wide, narrow = proj_in.shape[0], proj_out.shape[0]
    devices = lax.axis_size("ex")
    me = lax.axis_index("ex").astype(jnp.int32)
    simple = devices < 32 or devices & (devices - 1)
    if not simple:
        far = exchange(test_grads, devices // 2, devices)
    packed, grads = project(example_inputs, output_grads, proj_in, proj_out)
    if simple:
        packed = lax.psum(packed, "ex")
        pieces = [lax.all_gather(test_grads, "ex", axis=0, tiled=True)]
        sources = [list(range(devices))]
        me = me * 0
    else:
        packed, far = lax.optimization_barrier((packed, far))
        tests = jnp.concatenate([test_grads, far], axis=0)
        packed, pieces, sources = exchange_all(packed, tests, [0, devices // 2], devices)
    precond = precondition(packed, grads, examples * tokens * devices)
    scale = 4.0 / (wide * narrow * tokens) ** 0.5
    return score(me[None], precond, pieces, sources, scale)


def solution(mesh):
    return jax.shard_map(
        on_device,
        mesh=mesh,
        in_specs=(
            P(("grp", "ex"), None, None),
            P(("grp", "ex"), None, None),
            P(),
            P(),
            P("ex", None),
        ),
        out_specs=P(("grp", "ex"), None),
        check_vma=False,
    )
```

```python
import functools

import jax
import jax.numpy as jnp
from jax import lax
from jax.experimental import pallas as pl
from jax.experimental.pallas import tpu as pltpu
from jax.sharding import PartitionSpec as P

HIGHEST = lax.Precision.HIGHEST
DAMP = 0.1
DEPTH = 2
LONG = 10**10
VMEM = pltpu.MemorySpace.VMEM
SMEM = pltpu.MemorySpace.SMEM


def dot(a, b):
    return jnp.dot(a, b, preferred_element_type=jnp.float32)


def exact(a, b):
    return jnp.dot(a, b, precision=HIGHEST, preferred_element_type=jnp.float32)


def over_last(a, b):
    return lax.dot_general(a, b, (((1,), (1,)), ((), ())), preferred_element_type=jnp.float32)


def over_first(a, b):
    return lax.dot_general(a, b, (((0,), (0,)), ((), ())), preferred_element_type=jnp.float32)


def divisor(n, most):
    return max(d for d in range(1, most + 1) if n % d == 0)


def project_kernel(x_hbm, g_hbm, pin_hbm, pout_hbm, packed_ref, grads_ref, x, g, pin, pout, pin_t, both, sx, sg, sp):
    examples = x_hbm.shape[0]
    wide, narrow = pin.shape[0], pout.shape[0]
    chunks, rows = x.shape[:2]
    per = chunks // examples
    pin_copy = pltpu.make_async_copy(pin_hbm, pin, sp.at[0])
    pout_copy = pltpu.make_async_copy(pout_hbm, pout, sp.at[1])
    pin_copy.start()
    pout_copy.start()

    def place(i):
        return i // per, pl.ds(pl.multiple_of((i % per) * rows, rows), rows)

    def copies(i):
        return (
            pltpu.make_async_copy(x_hbm.at[place(i)], x.at[i], sx.at[i]),
            pltpu.make_async_copy(g_hbm.at[place(i)], g.at[i], sg.at[i]),
        )

    for i in range(min(DEPTH, chunks)):
        for copy in copies(i):
            copy.start()
    pin_copy.wait()
    pin_t[...] = pin[...].T
    pout_copy.wait()

    @pl.loop(0, chunks)
    def _(i):
        for copy in copies(i):
            copy.wait()

        @pl.when(i + DEPTH < chunks)
        def _():
            for copy in copies(i + DEPTH):
                copy.start()

        e, tokens = place(i)
        both[e, tokens, :wide] = dot(x[i], pin_t[...]).astype(jnp.bfloat16)
        both[e, tokens, wide:] = over_last(g[i], pout[...]).astype(jnp.bfloat16)

    for e in range(examples):
        sums = over_first(both[e], both[e])
        grads_ref[e] = sums[wide:, :wide]
        low = jnp.concatenate([sums[wide:, wide:], sums[narrow:wide, narrow:wide]], axis=1)
        if e == 0:
            packed_ref[:narrow] = sums[:narrow, :wide]
            packed_ref[narrow:] = low
        else:
            packed_ref[:narrow] += sums[:narrow, :wide]
            packed_ref[narrow:] += low


def project(x, g, pin, pout):
    examples, tokens, d = x.shape
    v = g.shape[2]
    wide, narrow = pin.shape[0], pout.shape[0]
    rows = divisor(tokens, 256)
    chunks = examples * (tokens // rows)
    return pl.pallas_call(
        project_kernel,
        out_shape=[
            pltpu.VMEM((wide, wide), jnp.float32),
            pltpu.VMEM((examples, narrow, wide), jnp.float32),
        ],
        in_specs=[pl.BlockSpec(memory_space=pl.ANY)] * 4,
        out_specs=[pl.BlockSpec(memory_space=VMEM)] * 2,
        scratch_shapes=[
            pltpu.VMEM((chunks, rows, d), x.dtype),
            pltpu.VMEM((chunks, rows, v), g.dtype),
            pltpu.VMEM((wide, d), pin.dtype),
            pltpu.VMEM((narrow, v), pout.dtype),
            pltpu.VMEM((d, wide), pin.dtype),
            pltpu.VMEM((examples, tokens, wide + narrow), jnp.bfloat16),
            pltpu.SemaphoreType.DMA((chunks,)),
            pltpu.SemaphoreType.DMA((chunks,)),
            pltpu.SemaphoreType.DMA((2,)),
        ],
        compiler_params=pltpu.CompilerParams(vmem_limit_bytes=60 * 2**20),
        name="project",
    )(x, g, pin, pout)


def factors(n):
    spread = n / (n + 2 * DAMP)
    result = []
    while spread > 2e-6:
        result.append(2 / (2 - spread * spread))
        spread = spread * spread / (2 - spread * spread)
    return result


def normalised(s):
    n = s.shape[0]
    eye = lax.broadcasted_iota(jnp.int32, (n, n), 0) == lax.broadcasted_iota(jnp.int32, (n, n), 1)
    diagonal = jnp.sum(jnp.where(eye, s, 0.0), axis=0, keepdims=True)
    mean = jnp.sum(diagonal, axis=1, keepdims=True) / n
    first = 2 / (n + 2 * DAMP)
    return (s / mean + jnp.where(eye, DAMP, 0.0)) * first, first / mean, eye


def precond_kernel(tokens, packed_ref, grads_ref, out_ref):
    wide = packed_ref.shape[0]
    examples, narrow, _ = grads_ref.shape
    packed = packed_ref[...]
    upper = packed[:narrow]
    lower = jnp.concatenate([upper[:, narrow:].T, packed[narrow:, narrow:]], axis=1)
    yi, scale_in, _ = normalised(jnp.concatenate([upper, lower], axis=0))
    yo, scale_out, eye = normalised(packed[narrow:, :narrow])
    w = grads_ref[...].reshape(examples * narrow, wide)
    xo = jnp.where(eye, 1.0, 0.0)
    wides, narrows = factors(wide), factors(narrow)
    for k in range(max(len(wides), len(narrows))):
        if k < len(wides):
            if k < len(wides) - 1:
                both = jnp.concatenate([yi, w], axis=0)
                both = wides[k] * (2 * both - exact(both, yi))
                yi, w = both[:wide], both[wide:]
            else:
                w = wides[k] * (2 * w - exact(w, yi))
        if k < len(narrows):
            if k < len(narrows) - 1:
                both = jnp.concatenate([yo, xo], axis=0)
                both = narrows[k] * (2 * both - exact(both, yo))
                yo, xo = both[:narrow], both[narrow:]
            else:
                xo = narrows[k] * (2 * xo - exact(xo, yo))
    scale = (scale_in * tokens) * (scale_out * tokens)
    for e in range(examples):
        both = exact(xo, w[e * narrow : (e + 1) * narrow]) * scale
        out_ref[e] = both.astype(jnp.bfloat16).astype(jnp.float32)


def precondition(packed, grads, tokens):
    return pl.pallas_call(
        functools.partial(precond_kernel, float(tokens)),
        out_shape=pltpu.VMEM(grads.shape, jnp.float32),
        in_specs=[pl.BlockSpec(memory_space=VMEM)] * 2,
        out_specs=pl.BlockSpec(memory_space=VMEM),
        name="precondition",
    )(*[pltpu.with_memory_space_constraint(a, VMEM) for a in (packed, grads)])


def score_kernel(sources, scale, me_ref, p_ref, *refs):
    pieces, out_ref = refs[:-1], refs[-1]
    examples, narrow, wide = p_ref.shape
    tests = out_ref.shape[1]
    me = me_ref[0]
    lane = lax.broadcasted_iota(jnp.int32, (1, tests), 1)
    for e in range(examples):

        def add(o, sums):
            p = p_ref[e, pl.ds(o, 1), :]
            here = pl.ds(pl.multiple_of(o * wide, wide), wide)
            return tuple(s + t[:, here].astype(jnp.float32) * p for s, t in zip(sums, pieces))

        zeros = tuple(jnp.zeros((t.shape[0], wide), jnp.float32) for t in pieces)
        sums = lax.fori_loop(0, narrow, add, zeros, unroll=4)
        total = jnp.zeros((1, tests), jnp.float32)
        for s, offsets in zip(sums, sources):
            rows = s.shape[0]
            per = rows // len(offsets)
            row = lax.broadcasted_iota(jnp.int32, (rows, 1), 0)
            target = jnp.zeros((rows, 1), jnp.int32)
            for i, offset in enumerate(offsets):
                inside = (row >= i * per) & (row < (i + 1) * per)
                target = jnp.where(inside, (me ^ offset) * per + row - i * per, target)
            by_row = jnp.sum(s, axis=1, keepdims=True)
            total += jnp.sum(jnp.where(target == lane, by_row, 0.0), axis=0, keepdims=True)
        out_ref[pl.ds(e, 1), :] = total * scale


def score(me, precond, pieces, sources, scale):
    tests = sum(t.shape[0] for t in pieces)
    return pl.pallas_call(
        functools.partial(score_kernel, sources, scale),
        out_shape=jax.ShapeDtypeStruct((precond.shape[0], tests), jnp.float32),
        in_specs=[pl.BlockSpec(memory_space=SMEM)] + [pl.BlockSpec(memory_space=VMEM)] * (1 + len(pieces)),
        out_specs=pl.BlockSpec(memory_space=VMEM),
        compiler_params=pltpu.CompilerParams(vmem_limit_bytes=32 * 2**20),
        name="score",
    )(me, *[pltpu.with_memory_space_constraint(a, VMEM) for a in (precond, *pieces)])


def exchange(x, bit, devices):
    return lax.ppermute(x, "ex", [(i, i ^ bit) for i in range(devices)])


def join(tests, offsets, bit, devices):
    both = jnp.concatenate([tests, exchange(tests, bit, devices)], axis=0)
    return both, offsets + [k ^ bit for k in offsets]


def add_kernel(a_ref, b_ref, out_ref):
    out_ref[...] = a_ref[...] + b_ref[...]


def add_late(a, b, flops=LONG):
    return pl.pallas_call(
        add_kernel,
        out_shape=pltpu.VMEM(a.shape, a.dtype),
        in_specs=[pl.BlockSpec(memory_space=VMEM)] * 2,
        out_specs=pl.BlockSpec(memory_space=VMEM),
        cost_estimate=pl.CostEstimate(flops=flops, bytes_accessed=3 * a.size * 4, transcendentals=0),
        name="add",
    )(*[pltpu.with_memory_space_constraint(t, VMEM) for t in (a, b)])


def exchange_all(packed, tests, offsets, devices):
    far = devices // 4
    packed, tests = lax.optimization_barrier((packed, tests))
    packed = packed + exchange(packed, 1, devices)
    packed = packed + exchange(packed, 2, devices)
    while far > 4:
        tests, offsets = join(tests, offsets, far, devices)
        far //= 2
    packed, tests = lax.optimization_barrier((packed, tests))
    half, rows = len(offsets) // 2, tests.shape[0] // 2
    a, a_off = exchange(tests, 2, devices), [k ^ 2 for k in offsets]
    b, b_off = exchange(tests, 4, devices), [k ^ 4 for k in offsets]
    packed = add_late(packed, exchange(packed, 8, devices))
    bit = 16
    while bit < devices:
        packed = packed + exchange(packed, bit, devices)
        bit *= 2
    c, c_off = exchange(b[:rows], 2, devices), [k ^ 2 for k in b_off[:half]]
    d, d_off = exchange(a[rows:], 4, devices), [k ^ 4 for k in a_off[half:]]
    packed = packed + exchange(packed, 4, devices)
    packed, c, d, tests, a, b = lax.optimization_barrier((packed, c, d, tests, a, b))
    everyone = jnp.concatenate([tests, a, b, c, d], axis=0)
    offsets = offsets + a_off + b_off + c_off + d_off
    pieces = [(everyone, offsets), (exchange(everyone, 1, devices), [k ^ 1 for k in offsets])]
    return packed, [t for t, _ in pieces], [off for _, off in pieces]


def on_device(example_inputs, output_grads, proj_in, proj_out, test_grads):
    examples, tokens, _ = example_inputs.shape
    wide, narrow = proj_in.shape[0], proj_out.shape[0]
    devices = lax.axis_size("ex")
    me = lax.axis_index("ex").astype(jnp.int32)
    simple = devices < 32 or devices & (devices - 1)
    if not simple:
        far = exchange(test_grads, devices // 2, devices)
    packed, grads = project(example_inputs, output_grads, proj_in, proj_out)
    if simple:
        packed = lax.psum(packed, "ex")
        pieces = [lax.all_gather(test_grads, "ex", axis=0, tiled=True)]
        sources = [list(range(devices))]
        me = me * 0
    else:
        packed, far = lax.optimization_barrier((packed, far))
        tests = jnp.concatenate([test_grads, far], axis=0)
        packed, pieces, sources = exchange_all(packed, tests, [0, devices // 2], devices)
    precond = precondition(packed, grads, examples * tokens * devices)
    scale = 4.0 / (wide * narrow * tokens) ** 0.5
    return score(me[None], precond, pieces, sources, scale)


def solution(mesh):
    return jax.shard_map(
        on_device,
        mesh=mesh,
        in_specs=(
            P(("grp", "ex"), None, None),
            P(("grp", "ex"), None, None),
            P(),
            P(),
            P("ex", None),
        ),
        out_specs=P(("grp", "ex"), None),
        check_vma=False,
    )
```

```python
import functools

import jax
import jax.numpy as jnp
from jax import lax
from jax.experimental import pallas as pl
from jax.experimental.pallas import tpu as pltpu
from jax.sharding import PartitionSpec as P

HIGHEST = lax.Precision.HIGHEST
DAMP = 0.1
DEPTH = 2
LONG = 10**10
VMEM = pltpu.MemorySpace.VMEM
SMEM = pltpu.MemorySpace.SMEM


def dot(a, b):
    return jnp.dot(a, b, preferred_element_type=jnp.float32)


def exact(a, b):
    return jnp.dot(a, b, precision=HIGHEST, preferred_element_type=jnp.float32)


def over_last(a, b):
    return lax.dot_general(a, b, (((1,), (1,)), ((), ())), preferred_element_type=jnp.float32)


def over_first(a, b):
    return lax.dot_general(a, b, (((0,), (0,)), ((), ())), preferred_element_type=jnp.float32)


def divisor(n, most):
    return max(d for d in range(1, most + 1) if n % d == 0)


def project_kernel(x_hbm, g_hbm, pin_hbm, pout_hbm, packed_ref, grads_ref, x, g, pin, pout, pin_t, both, sx, sg, sp):
    examples = x_hbm.shape[0]
    wide, narrow = pin.shape[0], pout.shape[0]
    chunks, rows = x.shape[:2]
    per = chunks // examples
    pin_copy = pltpu.make_async_copy(pin_hbm, pin, sp.at[0])
    pout_copy = pltpu.make_async_copy(pout_hbm, pout, sp.at[1])
    pin_copy.start()
    pout_copy.start()

    def place(i):
        return i // per, pl.ds(pl.multiple_of((i % per) * rows, rows), rows)

    def copies(i):
        return (
            pltpu.make_async_copy(x_hbm.at[place(i)], x.at[i], sx.at[i]),
            pltpu.make_async_copy(g_hbm.at[place(i)], g.at[i], sg.at[i]),
        )

    for i in range(min(DEPTH, chunks)):
        for copy in copies(i):
            copy.start()
    pin_copy.wait()
    pin_t[...] = pin[...].T
    pout_copy.wait()

    @pl.loop(0, chunks)
    def _(i):
        for copy in copies(i):
            copy.wait()

        @pl.when(i + DEPTH < chunks)
        def _():
            for copy in copies(i + DEPTH):
                copy.start()

        e, tokens = place(i)
        both[e, tokens, :wide] = dot(x[i], pin_t[...]).astype(jnp.bfloat16)
        both[e, tokens, wide:] = over_last(g[i], pout[...]).astype(jnp.bfloat16)

    total = jnp.zeros((wide + narrow, wide + narrow), jnp.float32)
    for e in range(examples):
        sums = over_first(both[e], both[e])
        grads_ref[e] = sums[wide:, :wide]
        total = total + sums
    row = lax.broadcasted_iota(jnp.int32, (narrow, narrow), 0)
    col = lax.broadcasted_iota(jnp.int32, (narrow, narrow), 1)
    small = total[wide:, wide:]
    diagonal = jnp.sum(jnp.where(row == col, small, 0.0), axis=0, keepdims=True)
    spare = jnp.where(row == narrow - 1, diagonal, diagonal[:, narrow - 1 :])
    packed_ref[:narrow, :narrow] = jnp.where(col < row, small, total[:narrow, :narrow])
    packed_ref[:narrow, narrow:] = jnp.where(col < row, spare, total[narrow:wide, narrow:wide])
    packed_ref[narrow:, :narrow] = total[: narrow // 2, narrow:wide]
    packed_ref[narrow:, narrow:] = total[narrow // 2 : narrow, narrow:wide]


def project(x, g, pin, pout):
    examples, tokens, d = x.shape
    v = g.shape[2]
    wide, narrow = pin.shape[0], pout.shape[0]
    rows = divisor(tokens, 256)
    chunks = examples * (tokens // rows)
    return pl.pallas_call(
        project_kernel,
        out_shape=[
            pltpu.VMEM((narrow + narrow // 2, wide), jnp.float32),
            pltpu.VMEM((examples, narrow, wide), jnp.float32),
        ],
        in_specs=[pl.BlockSpec(memory_space=pl.ANY)] * 4,
        out_specs=[pl.BlockSpec(memory_space=VMEM)] * 2,
        scratch_shapes=[
            pltpu.VMEM((chunks, rows, d), x.dtype),
            pltpu.VMEM((chunks, rows, v), g.dtype),
            pltpu.VMEM((wide, d), pin.dtype),
            pltpu.VMEM((narrow, v), pout.dtype),
            pltpu.VMEM((d, wide), pin.dtype),
            pltpu.VMEM((examples, tokens, wide + narrow), jnp.bfloat16),
            pltpu.SemaphoreType.DMA((chunks,)),
            pltpu.SemaphoreType.DMA((chunks,)),
            pltpu.SemaphoreType.DMA((2,)),
        ],
        compiler_params=pltpu.CompilerParams(vmem_limit_bytes=60 * 2**20),
        name="project",
    )(x, g, pin, pout)


def factors(n):
    spread = n / (n + 2 * DAMP)
    result = []
    while spread > 2e-6:
        result.append(2 / (2 - spread * spread))
        spread = spread * spread / (2 - spread * spread)
    return result


def normalised(s):
    n = s.shape[0]
    eye = lax.broadcasted_iota(jnp.int32, (n, n), 0) == lax.broadcasted_iota(jnp.int32, (n, n), 1)
    diagonal = jnp.sum(jnp.where(eye, s, 0.0), axis=0, keepdims=True)
    mean = jnp.sum(diagonal, axis=1, keepdims=True) / n
    first = 2 / (n + 2 * DAMP)
    return (s / mean + jnp.where(eye, DAMP, 0.0)) * first, first / mean, eye


def precond_kernel(tokens, packed_ref, grads_ref, out_ref):
    wide = packed_ref.shape[1]
    examples, narrow, _ = grads_ref.shape
    packed = packed_ref[...]
    row = lax.broadcasted_iota(jnp.int32, (narrow, narrow), 0)
    col = lax.broadcasted_iota(jnp.int32, (narrow, narrow), 1)
    left, right = packed[:narrow, :narrow], packed[:narrow, narrow:]
    corner = jnp.concatenate([packed[narrow:, :narrow], packed[narrow:, narrow:]], axis=0)
    zero = jnp.zeros((narrow, narrow), jnp.float32)
    above = jnp.concatenate(
        [
            jnp.concatenate([jnp.where(col > row, left, 0.0), corner], axis=1),
            jnp.concatenate([zero, jnp.where(col > row, right, 0.0)], axis=1),
        ],
        axis=0,
    )
    middle = jnp.concatenate(
        [
            jnp.concatenate([jnp.where(col == row, left, 0.0), zero], axis=1),
            jnp.concatenate([zero, jnp.where(col == row, right, 0.0)], axis=1),
        ],
        axis=0,
    )
    yi, scale_in, _ = normalised(above + above.T + middle)
    below = jnp.where(col < row, left, 0.0)
    diagonal = jnp.where(col[:1] < narrow - 1, right[narrow - 1 :], right[narrow - 2 : narrow - 1, :1])
    yo, scale_out, eye = normalised(below + below.T + jnp.where(col == row, diagonal, 0.0))
    w = grads_ref[...].reshape(examples * narrow, wide)
    xo = jnp.where(eye, 1.0, 0.0)
    wides, narrows = factors(wide), factors(narrow)
    for k in range(max(len(wides), len(narrows))):
        if k < len(wides):
            if k < len(wides) - 1:
                both = jnp.concatenate([yi, w], axis=0)
                both = wides[k] * (2 * both - exact(both, yi))
                yi, w = both[:wide], both[wide:]
            else:
                w = wides[k] * (2 * w - exact(w, yi))
        if k < len(narrows):
            if k < len(narrows) - 1:
                both = jnp.concatenate([yo, xo], axis=0)
                both = narrows[k] * (2 * both - exact(both, yo))
                yo, xo = both[:narrow], both[narrow:]
            else:
                xo = narrows[k] * (2 * xo - exact(xo, yo))
    scale = (scale_in * tokens) * (scale_out * tokens)
    for e in range(examples):
        both = exact(xo, w[e * narrow : (e + 1) * narrow]) * scale
        out_ref[e] = both.astype(jnp.bfloat16).astype(jnp.float32)


def precondition(packed, grads, tokens):
    return pl.pallas_call(
        functools.partial(precond_kernel, float(tokens)),
        out_shape=pltpu.VMEM(grads.shape, jnp.float32),
        in_specs=[pl.BlockSpec(memory_space=VMEM)] * 2,
        out_specs=pl.BlockSpec(memory_space=VMEM),
        name="precondition",
    )(*[pltpu.with_memory_space_constraint(a, VMEM) for a in (packed, grads)])


def score_kernel(sources, scale, me_ref, p_ref, *refs):
    pieces, out_ref = refs[:-1], refs[-1]
    examples, narrow, wide = p_ref.shape
    tests = out_ref.shape[1]
    me = me_ref[0]
    lane = lax.broadcasted_iota(jnp.int32, (1, tests), 1)
    for e in range(examples):

        def add(o, sums):
            p = p_ref[e, pl.ds(o, 1), :]
            here = pl.ds(pl.multiple_of(o * wide, wide), wide)
            return tuple(s + t[:, here].astype(jnp.float32) * p for s, t in zip(sums, pieces))

        zeros = tuple(jnp.zeros((t.shape[0], wide), jnp.float32) for t in pieces)
        sums = lax.fori_loop(0, narrow, add, zeros, unroll=4)
        total = jnp.zeros((1, tests), jnp.float32)
        for s, offsets in zip(sums, sources):
            rows = s.shape[0]
            per = rows // len(offsets)
            row = lax.broadcasted_iota(jnp.int32, (rows, 1), 0)
            target = jnp.zeros((rows, 1), jnp.int32)
            for i, offset in enumerate(offsets):
                inside = (row >= i * per) & (row < (i + 1) * per)
                target = jnp.where(inside, (me ^ offset) * per + row - i * per, target)
            by_row = jnp.sum(s, axis=1, keepdims=True)
            total += jnp.sum(jnp.where(target == lane, by_row, 0.0), axis=0, keepdims=True)
        out_ref[pl.ds(e, 1), :] = total * scale


def score(me, precond, pieces, sources, scale):
    tests = sum(t.shape[0] for t in pieces)
    return pl.pallas_call(
        functools.partial(score_kernel, sources, scale),
        out_shape=jax.ShapeDtypeStruct((precond.shape[0], tests), jnp.float32),
        in_specs=[pl.BlockSpec(memory_space=SMEM)] + [pl.BlockSpec(memory_space=VMEM)] * (1 + len(pieces)),
        out_specs=pl.BlockSpec(memory_space=VMEM),
        compiler_params=pltpu.CompilerParams(vmem_limit_bytes=32 * 2**20),
        name="score",
    )(me, *[pltpu.with_memory_space_constraint(a, VMEM) for a in (precond, *pieces)])


def exchange(x, bit, devices):
    return lax.ppermute(x, "ex", [(i, i ^ bit) for i in range(devices)])


def join(tests, offsets, bit, devices):
    both = jnp.concatenate([tests, exchange(tests, bit, devices)], axis=0)
    return both, offsets + [k ^ bit for k in offsets]


def add_kernel(a_ref, b_ref, out_ref):
    out_ref[...] = a_ref[...] + b_ref[...]


def add_late(a, b, flops=LONG):
    return pl.pallas_call(
        add_kernel,
        out_shape=pltpu.VMEM(a.shape, a.dtype),
        in_specs=[pl.BlockSpec(memory_space=VMEM)] * 2,
        out_specs=pl.BlockSpec(memory_space=VMEM),
        cost_estimate=pl.CostEstimate(flops=flops, bytes_accessed=3 * a.size * 4, transcendentals=0),
        name="add",
    )(*[pltpu.with_memory_space_constraint(t, VMEM) for t in (a, b)])


def exchange_all(packed, tests, offsets, devices):
    far = devices // 4
    packed, tests = lax.optimization_barrier((packed, tests))
    packed = packed + exchange(packed, 1, devices)
    packed = packed + exchange(packed, 2, devices)
    while far > 4:
        tests, offsets = join(tests, offsets, far, devices)
        far //= 2
    packed, tests = lax.optimization_barrier((packed, tests))
    half, rows = len(offsets) // 2, tests.shape[0] // 2
    a, a_off = exchange(tests, 2, devices), [k ^ 2 for k in offsets]
    b, b_off = exchange(tests, 4, devices), [k ^ 4 for k in offsets]
    packed = add_late(packed, exchange(packed, 8, devices))
    bit = 16
    while bit < devices:
        packed = add_late(packed, exchange(packed, bit, devices), LONG // 5)
        bit *= 2
    c, c_off = exchange(b[:rows], 2, devices), [k ^ 2 for k in b_off[:half]]
    d, d_off = exchange(a[rows:], 4, devices), [k ^ 4 for k in a_off[half:]]
    packed = packed + exchange(packed, 4, devices)
    packed, c, d, tests, a, b = lax.optimization_barrier((packed, c, d, tests, a, b))
    everyone = jnp.concatenate([tests, a, b, c, d], axis=0)
    offsets = offsets + a_off + b_off + c_off + d_off
    pieces = [(everyone, offsets), (exchange(everyone, 1, devices), [k ^ 1 for k in offsets])]
    return packed, [t for t, _ in pieces], [off for _, off in pieces]


def on_device(example_inputs, output_grads, proj_in, proj_out, test_grads):
    examples, tokens, _ = example_inputs.shape
    wide, narrow = proj_in.shape[0], proj_out.shape[0]
    devices = lax.axis_size("ex")
    me = lax.axis_index("ex").astype(jnp.int32)
    simple = devices < 32 or devices & (devices - 1)
    if not simple:
        far = exchange(test_grads, devices // 2, devices)
    packed, grads = project(example_inputs, output_grads, proj_in, proj_out)
    if simple:
        packed = lax.psum(packed, "ex")
        pieces = [lax.all_gather(test_grads, "ex", axis=0, tiled=True)]
        sources = [list(range(devices))]
        me = me * 0
    else:
        packed, far = lax.optimization_barrier((packed, far))
        tests = jnp.concatenate([test_grads, far], axis=0)
        packed, pieces, sources = exchange_all(packed, tests, [0, devices // 2], devices)
    precond = precondition(packed, grads, examples * tokens * devices)
    scale = 4.0 / (wide * narrow * tokens) ** 0.5
    return score(me[None], precond, pieces, sources, scale)


def solution(mesh):
    return jax.shard_map(
        on_device,
        mesh=mesh,
        in_specs=(
            P(("grp", "ex"), None, None),
            P(("grp", "ex"), None, None),
            P(),
            P(),
            P("ex", None),
        ),
        out_specs=P(("grp", "ex"), None),
        check_vma=False,
    )
```

```python
import functools

import jax
import jax.numpy as jnp
from jax import lax
from jax.experimental import pallas as pl
from jax.experimental.pallas import tpu as pltpu
from jax.sharding import PartitionSpec as P

HIGHEST = lax.Precision.HIGHEST
DAMP = 0.1
DEPTH = 2
LONG = 10**10
VMEM = pltpu.MemorySpace.VMEM
SMEM = pltpu.MemorySpace.SMEM


def dot(a, b):
    return jnp.dot(a, b, preferred_element_type=jnp.float32)


def exact(a, b):
    return jnp.dot(a, b, precision=HIGHEST, preferred_element_type=jnp.float32)


def over_last(a, b):
    return lax.dot_general(a, b, (((1,), (1,)), ((), ())), preferred_element_type=jnp.float32)


def over_first(a, b):
    return lax.dot_general(a, b, (((0,), (0,)), ((), ())), preferred_element_type=jnp.float32)


def divisor(n, most):
    return max(d for d in range(1, most + 1) if n % d == 0)


def project_kernel(x_hbm, g_hbm, pin_hbm, pout_hbm, packed_ref, grads_ref, x, g, pin, pout, pin_t, both, sx, sg, sp):
    examples = x_hbm.shape[0]
    wide, narrow = pin.shape[0], pout.shape[0]
    chunks, rows = x.shape[:2]
    per = chunks // examples
    pin_copy = pltpu.make_async_copy(pin_hbm, pin, sp.at[0])
    pout_copy = pltpu.make_async_copy(pout_hbm, pout, sp.at[1])
    pin_copy.start()
    pout_copy.start()

    def place(i):
        return i // per, pl.ds((i % per) * rows, rows)

    def copies(i):
        return (
            pltpu.make_async_copy(x_hbm.at[place(i)], x.at[i], sx.at[i]),
            pltpu.make_async_copy(g_hbm.at[place(i)], g.at[i], sg.at[i]),
        )

    for i in range(min(DEPTH, chunks)):
        for copy in copies(i):
            copy.start()
    pin_copy.wait()
    if DEPTH < chunks:
        for copy in copies(DEPTH):
            copy.start()
    pin_t[...] = pin[...].T
    pout_copy.wait()

    for i in range(chunks):
        for copy in copies(i):
            copy.wait()

        if i + DEPTH + 1 < chunks:
            for copy in copies(i + DEPTH + 1):
                copy.start()

        e, tokens = place(i)
        both[e, tokens, :wide] = dot(x[i], pin_t[...]).astype(jnp.bfloat16)
        both[e, tokens, wide:] = over_last(g[i], pout[...]).astype(jnp.bfloat16)

    total = jnp.zeros((wide + narrow, wide + narrow), jnp.float32)
    for e in range(examples):
        sums = over_first(both[e], both[e])
        grads_ref[e] = sums[wide:, :wide]
        total = total + sums
    row = lax.broadcasted_iota(jnp.int32, (narrow, narrow), 0)
    col = lax.broadcasted_iota(jnp.int32, (narrow, narrow), 1)
    small = total[wide:, wide:]
    diagonal = jnp.sum(jnp.where(row == col, small, 0.0), axis=0, keepdims=True)
    spare = jnp.where(row == narrow - 1, diagonal, diagonal[:, narrow - 1 :])
    packed_ref[:narrow, :narrow] = jnp.where(col < row, small, total[:narrow, :narrow])
    packed_ref[:narrow, narrow:] = jnp.where(col < row, spare, total[narrow:wide, narrow:wide])
    packed_ref[narrow:, :narrow] = total[: narrow // 2, narrow:wide]
    packed_ref[narrow:, narrow:] = total[narrow // 2 : narrow, narrow:wide]


def project(x, g, pin, pout):
    examples, tokens, d = x.shape
    v = g.shape[2]
    wide, narrow = pin.shape[0], pout.shape[0]
    rows = divisor(tokens, 256)
    chunks = examples * (tokens // rows)
    return pl.pallas_call(
        project_kernel,
        out_shape=[
            pltpu.VMEM((narrow + narrow // 2, wide), jnp.float32),
            pltpu.VMEM((examples, narrow, wide), jnp.float32),
        ],
        in_specs=[pl.BlockSpec(memory_space=pl.ANY)] * 4,
        out_specs=[pl.BlockSpec(memory_space=VMEM)] * 2,
        scratch_shapes=[
            pltpu.VMEM((chunks, rows, d), x.dtype),
            pltpu.VMEM((chunks, rows, v), g.dtype),
            pltpu.VMEM((wide, d), pin.dtype),
            pltpu.VMEM((narrow, v), pout.dtype),
            pltpu.VMEM((d, wide), pin.dtype),
            pltpu.VMEM((examples, tokens, wide + narrow), jnp.bfloat16),
            pltpu.SemaphoreType.DMA((chunks,)),
            pltpu.SemaphoreType.DMA((chunks,)),
            pltpu.SemaphoreType.DMA((2,)),
        ],
        compiler_params=pltpu.CompilerParams(vmem_limit_bytes=60 * 2**20),
        name="project",
    )(x, g, pin, pout)


def factors(n):
    spread = n / (n + 2 * DAMP)
    result = []
    while spread > 2e-6:
        result.append(2 / (2 - spread * spread))
        spread = spread * spread / (2 - spread * spread)
    return result


def normalised(s):
    n = s.shape[0]
    eye = lax.broadcasted_iota(jnp.int32, (n, n), 0) == lax.broadcasted_iota(jnp.int32, (n, n), 1)
    diagonal = jnp.sum(jnp.where(eye, s, 0.0), axis=0, keepdims=True)
    mean = jnp.sum(diagonal, axis=1, keepdims=True) / n
    first = 2 / (n + 2 * DAMP)
    return (s / mean + jnp.where(eye, DAMP, 0.0)) * first, first / mean, eye


def precond_kernel(tokens, packed_ref, grads_ref, out_ref):
    wide = packed_ref.shape[1]
    examples, narrow, _ = grads_ref.shape
    packed = packed_ref[...]
    row = lax.broadcasted_iota(jnp.int32, (narrow, narrow), 0)
    col = lax.broadcasted_iota(jnp.int32, (narrow, narrow), 1)
    left, right = packed[:narrow, :narrow], packed[:narrow, narrow:]
    corner = jnp.concatenate([packed[narrow:, :narrow], packed[narrow:, narrow:]], axis=0)
    zero = jnp.zeros((narrow, narrow), jnp.float32)
    above = jnp.concatenate(
        [
            jnp.concatenate([jnp.where(col > row, left, 0.0), corner], axis=1),
            jnp.concatenate([zero, jnp.where(col > row, right, 0.0)], axis=1),
        ],
        axis=0,
    )
    middle = jnp.concatenate(
        [
            jnp.concatenate([jnp.where(col == row, left, 0.0), zero], axis=1),
            jnp.concatenate([zero, jnp.where(col == row, right, 0.0)], axis=1),
        ],
        axis=0,
    )
    yi, scale_in, _ = normalised(above + above.T + middle)
    below = jnp.where(col < row, left, 0.0)
    diagonal = jnp.where(col[:1] < narrow - 1, right[narrow - 1 :], right[narrow - 2 : narrow - 1, :1])
    yo, scale_out, eye = normalised(below + below.T + jnp.where(col == row, diagonal, 0.0))
    w = grads_ref[...].reshape(examples * narrow, wide)
    xo = jnp.where(eye, 1.0, 0.0)
    wides, narrows = factors(wide), factors(narrow)
    for k in range(max(len(wides), len(narrows))):
        if k < len(wides):
            if k < len(wides) - 1:
                both = jnp.concatenate([yi, w], axis=0)
                both = wides[k] * (2 * both - exact(both, yi))
                yi, w = both[:wide], both[wide:]
            else:
                w = wides[k] * (2 * w - exact(w, yi))
        if k < len(narrows):
            if k < len(narrows) - 1:
                both = jnp.concatenate([yo, xo], axis=0)
                both = narrows[k] * (2 * both - exact(both, yo))
                yo, xo = both[:narrow], both[narrow:]
            else:
                xo = narrows[k] * (2 * xo - exact(xo, yo))
    scale = (scale_in * tokens) * (scale_out * tokens)
    for e in range(examples):
        both = exact(xo, w[e * narrow : (e + 1) * narrow]) * scale
        out_ref[e] = both.astype(jnp.bfloat16).astype(jnp.float32)


def precondition(packed, grads, tokens):
    return pl.pallas_call(
        functools.partial(precond_kernel, float(tokens)),
        out_shape=pltpu.VMEM(grads.shape, jnp.float32),
        in_specs=[pl.BlockSpec(memory_space=VMEM)] * 2,
        out_specs=pl.BlockSpec(memory_space=VMEM),
        name="precondition",
    )(*[pltpu.with_memory_space_constraint(a, VMEM) for a in (packed, grads)])


def score_kernel(sources, scale, me_ref, p_ref, *refs):
    pieces, out_ref = refs[:-1], refs[-1]
    examples, narrow, wide = p_ref.shape
    tests = out_ref.shape[1]
    me = me_ref[0]
    lane = lax.broadcasted_iota(jnp.int32, (1, tests), 1)
    for e in range(examples):
        sums = [jnp.zeros((t.shape[0], wide), jnp.float32) for t in pieces]
        for o in range(narrow):
            p = p_ref[e, o : o + 1, :]
            here = slice(o * wide, (o + 1) * wide)
            sums = [s + t[:, here].astype(jnp.float32) * p for s, t in zip(sums, pieces)]
        total = jnp.zeros((1, tests), jnp.float32)
        for s, offsets in zip(sums, sources):
            rows = s.shape[0]
            per = rows // len(offsets)
            row = lax.broadcasted_iota(jnp.int32, (rows, 1), 0)
            target = jnp.zeros((rows, 1), jnp.int32)
            for i, offset in enumerate(offsets):
                inside = (row >= i * per) & (row < (i + 1) * per)
                target = jnp.where(inside, (me ^ offset) * per + row - i * per, target)
            by_row = jnp.sum(s, axis=1, keepdims=True)
            total += jnp.sum(jnp.where(target == lane, by_row, 0.0), axis=0, keepdims=True)
        out_ref[pl.ds(e, 1), :] = total * scale


def score(me, precond, pieces, sources, scale):
    tests = sum(t.shape[0] for t in pieces)
    return pl.pallas_call(
        functools.partial(score_kernel, sources, scale),
        out_shape=jax.ShapeDtypeStruct((precond.shape[0], tests), jnp.float32),
        in_specs=[pl.BlockSpec(memory_space=SMEM)] + [pl.BlockSpec(memory_space=VMEM)] * (1 + len(pieces)),
        out_specs=pl.BlockSpec(memory_space=VMEM),
        compiler_params=pltpu.CompilerParams(vmem_limit_bytes=32 * 2**20),
        name="score",
    )(me, *[pltpu.with_memory_space_constraint(a, VMEM) for a in (precond, *pieces)])


def exchange(x, bit, devices):
    return lax.ppermute(x, "ex", [(i, i ^ bit) for i in range(devices)])


def join(tests, offsets, bit, devices):
    both = jnp.concatenate([tests, exchange(tests, bit, devices)], axis=0)
    return both, offsets + [k ^ bit for k in offsets]


def add_kernel(a_ref, b_ref, out_ref):
    out_ref[...] = a_ref[...] + b_ref[...]


def add_late(a, b, flops=LONG):
    return pl.pallas_call(
        add_kernel,
        out_shape=pltpu.VMEM(a.shape, a.dtype),
        in_specs=[pl.BlockSpec(memory_space=VMEM)] * 2,
        out_specs=pl.BlockSpec(memory_space=VMEM),
        cost_estimate=pl.CostEstimate(flops=flops, bytes_accessed=3 * a.size * 4, transcendentals=0),
        name="add",
    )(*[pltpu.with_memory_space_constraint(t, VMEM) for t in (a, b)])


def exchange_all(packed, tests, offsets, devices):
    far = devices // 4
    packed, tests = lax.optimization_barrier((packed, tests))
    packed = packed + exchange(packed, 1, devices)
    packed = packed + exchange(packed, 2, devices)
    while far > 4:
        tests, offsets = join(tests, offsets, far, devices)
        far //= 2
    packed, tests = lax.optimization_barrier((packed, tests))
    half, rows = len(offsets) // 2, tests.shape[0] // 2
    a, a_off = exchange(tests, 2, devices), [k ^ 2 for k in offsets]
    b, b_off = exchange(tests, 4, devices), [k ^ 4 for k in offsets]
    packed = add_late(packed, exchange(packed, 8, devices))
    bit = 16
    while bit < devices:
        packed = add_late(packed, exchange(packed, bit, devices), LONG // 5)
        bit *= 2
    c, c_off = exchange(b[:rows], 2, devices), [k ^ 2 for k in b_off[:half]]
    d, d_off = exchange(a[rows:], 4, devices), [k ^ 4 for k in a_off[half:]]
    packed = packed + exchange(packed, 4, devices)
    packed, c, d, tests, a, b = lax.optimization_barrier((packed, c, d, tests, a, b))
    everyone = jnp.concatenate([tests, a, b, c, d], axis=0)
    offsets = offsets + a_off + b_off + c_off + d_off
    pieces = [(everyone, offsets), (exchange(everyone, 1, devices), [k ^ 1 for k in offsets])]
    return packed, [t for t, _ in pieces], [off for _, off in pieces]


def on_device(example_inputs, output_grads, proj_in, proj_out, test_grads):
    examples, tokens, _ = example_inputs.shape
    wide, narrow = proj_in.shape[0], proj_out.shape[0]
    devices = lax.axis_size("ex")
    me = lax.axis_index("ex").astype(jnp.int32)
    simple = devices < 32 or devices & (devices - 1)
    if not simple:
        far = exchange(test_grads, devices // 2, devices)
    packed, grads = project(example_inputs, output_grads, proj_in, proj_out)
    if simple:
        packed = lax.psum(packed, "ex")
        pieces = [lax.all_gather(test_grads, "ex", axis=0, tiled=True)]
        sources = [list(range(devices))]
        me = me * 0
    else:
        packed, far = lax.optimization_barrier((packed, far))
        tests = jnp.concatenate([test_grads, far], axis=0)
        packed, pieces, sources = exchange_all(packed, tests, [0, devices // 2], devices)
    precond = precondition(packed, grads, examples * tokens * devices)
    scale = 4.0 / (wide * narrow * tokens) ** 0.5
    return score(me[None], precond, pieces, sources, scale)


def solution(mesh):
    return jax.shard_map(
        on_device,
        mesh=mesh,
        in_specs=(
            P(("grp", "ex"), None, None),
            P(("grp", "ex"), None, None),
            P(),
            P(),
            P("ex", None),
        ),
        out_specs=P(("grp", "ex"), None),
        check_vma=False,
    )
```

```python
import functools

import jax
import jax.numpy as jnp
from jax import lax
from jax.experimental import pallas as pl
from jax.experimental.pallas import tpu as pltpu
from jax.sharding import PartitionSpec as P

HIGHEST = lax.Precision.HIGHEST
DAMP = 0.1
DEPTH = 2
LONG = 10**10
VMEM = pltpu.MemorySpace.VMEM
SMEM = pltpu.MemorySpace.SMEM


def dot(a, b):
    return jnp.dot(a, b, preferred_element_type=jnp.float32)


def exact(a, b):
    return jnp.dot(a, b, precision=HIGHEST, preferred_element_type=jnp.float32)


def halves(a):
    high = a.astype(jnp.bfloat16)
    return high, (a - high.astype(jnp.float32)).astype(jnp.bfloat16)


def near_exact(a, b):
    (a_high, a_low), (b_high, b_low) = halves(a), halves(b)
    return dot(a_high, b_high) + (dot(a_low, b_high) + dot(a_high, b_low))


def over_last(a, b):
    return lax.dot_general(a, b, (((1,), (1,)), ((), ())), preferred_element_type=jnp.float32)


def over_first(a, b):
    return lax.dot_general(a, b, (((0,), (0,)), ((), ())), preferred_element_type=jnp.float32)


def divisor(n, most):
    return max(d for d in range(1, most + 1) if n % d == 0)


def project_kernel(x_hbm, g_hbm, pin_hbm, pout_hbm, packed_ref, grads_ref, x, g, pin, pout, pin_t, both, sx, sg, sp):
    examples = x_hbm.shape[0]
    wide, narrow = pin.shape[0], pout.shape[0]
    chunks, rows = x.shape[:2]
    per = chunks // examples
    pin_copy = pltpu.make_async_copy(pin_hbm, pin, sp.at[0])
    pout_copy = pltpu.make_async_copy(pout_hbm, pout, sp.at[1])
    pin_copy.start()
    pout_copy.start()

    def place(i):
        return i // per, pl.ds((i % per) * rows, rows)

    def copies(i):
        return (
            pltpu.make_async_copy(x_hbm.at[place(i)], x.at[i], sx.at[i]),
            pltpu.make_async_copy(g_hbm.at[place(i)], g.at[i], sg.at[i]),
        )

    for i in range(min(DEPTH, chunks)):
        for copy in copies(i):
            copy.start()
    pin_copy.wait()
    if DEPTH < chunks:
        for copy in copies(DEPTH):
            copy.start()
    pin_t[...] = pin[...].T
    pout_copy.wait()

    for i in range(chunks):
        for copy in copies(i):
            copy.wait()

        if i + DEPTH + 1 < chunks:
            for copy in copies(i + DEPTH + 1):
                copy.start()

        e, tokens = place(i)
        both[e, tokens, :wide] = dot(x[i], pin_t[...]).astype(jnp.bfloat16)
        both[e, tokens, wide:] = over_last(g[i], pout[...]).astype(jnp.bfloat16)

    total = jnp.zeros((wide + narrow, wide + narrow), jnp.float32)
    for e in range(examples):
        sums = over_first(both[e], both[e])
        grads_ref[e] = sums[wide:, :wide]
        total = total + sums
    row = lax.broadcasted_iota(jnp.int32, (narrow, narrow), 0)
    col = lax.broadcasted_iota(jnp.int32, (narrow, narrow), 1)
    small = total[wide:, wide:]
    diagonal = jnp.sum(jnp.where(row == col, small, 0.0), axis=0, keepdims=True)
    spare = jnp.where(row == narrow - 1, diagonal, diagonal[:, narrow - 1 :])
    packed_ref[:narrow, :narrow] = jnp.where(col < row, small, total[:narrow, :narrow])
    packed_ref[:narrow, narrow:] = jnp.where(col < row, spare, total[narrow:wide, narrow:wide])
    packed_ref[narrow:, :narrow] = total[: narrow // 2, narrow:wide]
    packed_ref[narrow:, narrow:] = total[narrow // 2 : narrow, narrow:wide]


def project(x, g, pin, pout):
    examples, tokens, d = x.shape
    v = g.shape[2]
    wide, narrow = pin.shape[0], pout.shape[0]
    rows = divisor(tokens, 256)
    chunks = examples * (tokens // rows)
    return pl.pallas_call(
        project_kernel,
        out_shape=[
            pltpu.VMEM((narrow + narrow // 2, wide), jnp.float32),
            pltpu.VMEM((examples, narrow, wide), jnp.float32),
        ],
        in_specs=[pl.BlockSpec(memory_space=pl.ANY)] * 4,
        out_specs=[pl.BlockSpec(memory_space=VMEM)] * 2,
        scratch_shapes=[
            pltpu.VMEM((chunks, rows, d), x.dtype),
            pltpu.VMEM((chunks, rows, v), g.dtype),
            pltpu.VMEM((wide, d), pin.dtype),
            pltpu.VMEM((narrow, v), pout.dtype),
            pltpu.VMEM((d, wide), pin.dtype),
            pltpu.VMEM((examples, tokens, wide + narrow), jnp.bfloat16),
            pltpu.SemaphoreType.DMA((chunks,)),
            pltpu.SemaphoreType.DMA((chunks,)),
            pltpu.SemaphoreType.DMA((2,)),
        ],
        compiler_params=pltpu.CompilerParams(vmem_limit_bytes=60 * 2**20),
        name="project",
    )(x, g, pin, pout)


def factors(n):
    spread = n / (n + 2 * DAMP)
    result = []
    while spread > 2e-6:
        result.append(2 / (2 - spread * spread))
        spread = spread * spread / (2 - spread * spread)
    return result


def normalised(s):
    n = s.shape[0]
    eye = lax.broadcasted_iota(jnp.int32, (n, n), 0) == lax.broadcasted_iota(jnp.int32, (n, n), 1)
    diagonal = jnp.sum(jnp.where(eye, s, 0.0), axis=0, keepdims=True)
    mean = jnp.sum(diagonal, axis=1, keepdims=True) / n
    first = 2 / (n + 2 * DAMP)
    return (s / mean + jnp.where(eye, DAMP, 0.0)) * first, first / mean, eye


def precond_kernel(tokens, packed_ref, grads_ref, out_ref):
    wide = packed_ref.shape[1]
    examples, narrow, _ = grads_ref.shape
    packed = packed_ref[...]
    row = lax.broadcasted_iota(jnp.int32, (narrow, narrow), 0)
    col = lax.broadcasted_iota(jnp.int32, (narrow, narrow), 1)
    left, right = packed[:narrow, :narrow], packed[:narrow, narrow:]
    corner = jnp.concatenate([packed[narrow:, :narrow], packed[narrow:, narrow:]], axis=0)
    zero = jnp.zeros((narrow, narrow), jnp.float32)
    above = jnp.concatenate(
        [
            jnp.concatenate([jnp.where(col > row, left, 0.0), corner], axis=1),
            jnp.concatenate([zero, jnp.where(col > row, right, 0.0)], axis=1),
        ],
        axis=0,
    )
    middle = jnp.concatenate(
        [
            jnp.concatenate([jnp.where(col == row, left, 0.0), zero], axis=1),
            jnp.concatenate([zero, jnp.where(col == row, right, 0.0)], axis=1),
        ],
        axis=0,
    )
    yi, scale_in, _ = normalised(above + above.T + middle)
    below = jnp.where(col < row, left, 0.0)
    diagonal = jnp.where(col[:1] < narrow - 1, right[narrow - 1 :], right[narrow - 2 : narrow - 1, :1])
    yo, scale_out, eye = normalised(below + below.T + jnp.where(col == row, diagonal, 0.0))
    w = grads_ref[...].reshape(examples * narrow, wide)
    xo = jnp.where(eye, 1.0, 0.0)
    wides, narrows = factors(wide), factors(narrow)
    for k in range(max(len(wides), len(narrows))):
        times = exact if k < 5 else near_exact
        if k < len(wides):
            if k < len(wides) - 1:
                both = jnp.concatenate([yi, w], axis=0)
                both = wides[k] * (2 * both - times(both, yi))
                yi, w = both[:wide], both[wide:]
            else:
                w = wides[k] * (2 * w - times(w, yi))
        if k < len(narrows):
            if k < len(narrows) - 1:
                both = jnp.concatenate([yo, xo], axis=0)
                both = narrows[k] * (2 * both - times(both, yo))
                yo, xo = both[:narrow], both[narrow:]
            else:
                xo = narrows[k] * (2 * xo - times(xo, yo))
    scale = (scale_in * tokens) * (scale_out * tokens)
    for e in range(examples):
        both = near_exact(xo, w[e * narrow : (e + 1) * narrow]) * scale
        out_ref[e] = both.astype(jnp.bfloat16).astype(jnp.float32)


def precondition(packed, grads, tokens):
    return pl.pallas_call(
        functools.partial(precond_kernel, float(tokens)),
        out_shape=pltpu.VMEM(grads.shape, jnp.float32),
        in_specs=[pl.BlockSpec(memory_space=VMEM)] * 2,
        out_specs=pl.BlockSpec(memory_space=VMEM),
        name="precondition",
    )(*[pltpu.with_memory_space_constraint(a, VMEM) for a in (packed, grads)])


def score_kernel(sources, scale, me_ref, p_ref, *refs):
    pieces, out_ref = refs[:-1], refs[-1]
    examples, narrow, wide = p_ref.shape
    tests = out_ref.shape[1]
    me = me_ref[0]
    lane = lax.broadcasted_iota(jnp.int32, (1, tests), 1)
    for e in range(examples):
        sums = [jnp.zeros((t.shape[0], wide), jnp.float32) for t in pieces]
        for o in range(narrow):
            p = p_ref[e, o : o + 1, :]
            here = slice(o * wide, (o + 1) * wide)
            sums = [s + t[:, here].astype(jnp.float32) * p for s, t in zip(sums, pieces)]
        total = jnp.zeros((1, tests), jnp.float32)
        for s, offsets in zip(sums, sources):
            rows = s.shape[0]
            per = rows // len(offsets)
            row = lax.broadcasted_iota(jnp.int32, (rows, 1), 0)
            target = jnp.zeros((rows, 1), jnp.int32)
            for i, offset in enumerate(offsets):
                inside = (row >= i * per) & (row < (i + 1) * per)
                target = jnp.where(inside, (me ^ offset) * per + row - i * per, target)
            by_row = jnp.sum(s, axis=1, keepdims=True)
            total += jnp.sum(jnp.where(target == lane, by_row, 0.0), axis=0, keepdims=True)
        out_ref[pl.ds(e, 1), :] = total * scale


def score(me, precond, pieces, sources, scale):
    tests = sum(t.shape[0] for t in pieces)
    return pl.pallas_call(
        functools.partial(score_kernel, sources, scale),
        out_shape=jax.ShapeDtypeStruct((precond.shape[0], tests), jnp.float32),
        in_specs=[pl.BlockSpec(memory_space=SMEM)] + [pl.BlockSpec(memory_space=VMEM)] * (1 + len(pieces)),
        out_specs=pl.BlockSpec(memory_space=VMEM),
        compiler_params=pltpu.CompilerParams(vmem_limit_bytes=32 * 2**20),
        name="score",
    )(me, *[pltpu.with_memory_space_constraint(a, VMEM) for a in (precond, *pieces)])


def exchange(x, bit, devices):
    return lax.ppermute(x, "ex", [(i, i ^ bit) for i in range(devices)])


def join(tests, offsets, bit, devices):
    both = jnp.concatenate([tests, exchange(tests, bit, devices)], axis=0)
    return both, offsets + [k ^ bit for k in offsets]


def add_kernel(a_ref, b_ref, out_ref):
    out_ref[...] = a_ref[...] + b_ref[...]


def add_late(a, b, flops=LONG):
    return pl.pallas_call(
        add_kernel,
        out_shape=pltpu.VMEM(a.shape, a.dtype),
        in_specs=[pl.BlockSpec(memory_space=VMEM)] * 2,
        out_specs=pl.BlockSpec(memory_space=VMEM),
        cost_estimate=pl.CostEstimate(flops=flops, bytes_accessed=3 * a.size * 4, transcendentals=0),
        name="add",
    )(*[pltpu.with_memory_space_constraint(t, VMEM) for t in (a, b)])


def exchange_all(packed, tests, offsets, devices):
    far = devices // 4
    packed, tests = lax.optimization_barrier((packed, tests))
    packed = packed + exchange(packed, 1, devices)
    packed = packed + exchange(packed, 2, devices)
    while far > 4:
        tests, offsets = join(tests, offsets, far, devices)
        far //= 2
    packed, tests = lax.optimization_barrier((packed, tests))
    half, rows = len(offsets) // 2, tests.shape[0] // 2
    a, a_off = exchange(tests, 2, devices), [k ^ 2 for k in offsets]
    b, b_off = exchange(tests, 4, devices), [k ^ 4 for k in offsets]
    packed = add_late(packed, exchange(packed, 8, devices))
    bit = 16
    while bit < devices:
        packed = add_late(packed, exchange(packed, bit, devices), LONG // 5)
        bit *= 2
    c, c_off = exchange(b[:rows], 2, devices), [k ^ 2 for k in b_off[:half]]
    d, d_off = exchange(a[rows:], 4, devices), [k ^ 4 for k in a_off[half:]]
    packed = packed + exchange(packed, 4, devices)
    packed, c, d, tests, a, b = lax.optimization_barrier((packed, c, d, tests, a, b))
    everyone = jnp.concatenate([tests, a, b, c, d], axis=0)
    offsets = offsets + a_off + b_off + c_off + d_off
    pieces = [(everyone, offsets), (exchange(everyone, 1, devices), [k ^ 1 for k in offsets])]
    return packed, [t for t, _ in pieces], [off for _, off in pieces]


def on_device(example_inputs, output_grads, proj_in, proj_out, test_grads):
    examples, tokens, _ = example_inputs.shape
    wide, narrow = proj_in.shape[0], proj_out.shape[0]
    devices = lax.axis_size("ex")
    me = lax.axis_index("ex").astype(jnp.int32)
    simple = devices < 32 or devices & (devices - 1)
    if not simple:
        far = exchange(test_grads, devices // 2, devices)
    packed, grads = project(example_inputs, output_grads, proj_in, proj_out)
    if simple:
        packed = lax.psum(packed, "ex")
        pieces = [lax.all_gather(test_grads, "ex", axis=0, tiled=True)]
        sources = [list(range(devices))]
        me = me * 0
    else:
        packed, far = lax.optimization_barrier((packed, far))
        tests = jnp.concatenate([test_grads, far], axis=0)
        packed, pieces, sources = exchange_all(packed, tests, [0, devices // 2], devices)
    precond = precondition(packed, grads, examples * tokens * devices)
    scale = 4.0 / (wide * narrow * tokens) ** 0.5
    return score(me[None], precond, pieces, sources, scale)


def solution(mesh):
    return jax.shard_map(
        on_device,
        mesh=mesh,
        in_specs=(
            P(("grp", "ex"), None, None),
            P(("grp", "ex"), None, None),
            P(),
            P(),
            P("ex", None),
        ),
        out_specs=P(("grp", "ex"), None),
        check_vma=False,
    )
```

```python
import functools

import jax
import jax.numpy as jnp
from jax import lax
from jax.experimental import pallas as pl
from jax.experimental.pallas import tpu as pltpu
from jax.sharding import PartitionSpec as P

HIGHEST = lax.Precision.HIGHEST
DAMP = 0.1
DEPTH = 2
LONG = 10**10
VMEM = pltpu.MemorySpace.VMEM
SMEM = pltpu.MemorySpace.SMEM


def dot(a, b):
    return jnp.dot(a, b, preferred_element_type=jnp.float32)


def exact(a, b):
    return jnp.dot(a, b, precision=HIGHEST, preferred_element_type=jnp.float32)


def halves(a):
    high = a.astype(jnp.bfloat16)
    return high, (a - high.astype(jnp.float32)).astype(jnp.bfloat16)


def near_exact(a, b):
    (a_high, a_low), (b_high, b_low) = halves(a), halves(b)
    return dot(a_high, b_high) + (dot(a_low, b_high) + dot(a_high, b_low))


def over_last(a, b):
    return lax.dot_general(a, b, (((1,), (1,)), ((), ())), preferred_element_type=jnp.float32)


def over_first(a, b):
    return lax.dot_general(a, b, (((0,), (0,)), ((), ())), preferred_element_type=jnp.float32)


def divisor(n, most):
    return max(d for d in range(1, most + 1) if n % d == 0)


def project_kernel(x_hbm, g_hbm, pin_hbm, pout_hbm, packed_ref, grads_ref, x, g, pin, pout, pin_t, both, sx, sg, sp):
    examples = x_hbm.shape[0]
    wide, narrow = pin.shape[0], pout.shape[0]
    chunks, rows = x.shape[:2]
    per = chunks // examples
    pin_copy = pltpu.make_async_copy(pin_hbm, pin, sp.at[0])
    pout_copy = pltpu.make_async_copy(pout_hbm, pout, sp.at[1])
    pin_copy.start()
    pout_copy.start()

    def place(i):
        return i // per, pl.ds((i % per) * rows, rows)

    def copies(i):
        return (
            pltpu.make_async_copy(x_hbm.at[place(i)], x.at[i], sx.at[i]),
            pltpu.make_async_copy(g_hbm.at[place(i)], g.at[i], sg.at[i]),
        )

    for i in range(min(DEPTH, chunks)):
        for copy in copies(i):
            copy.start()
    pin_copy.wait()
    if DEPTH < chunks:
        for copy in copies(DEPTH):
            copy.start()
    pin_t[...] = pin[...].T
    pout_copy.wait()

    for i in range(chunks):
        for copy in copies(i):
            copy.wait()

        if i + DEPTH + 1 < chunks:
            for copy in copies(i + DEPTH + 1):
                copy.start()

        e, tokens = place(i)
        both[e, tokens, :wide] = dot(x[i], pin_t[...]).astype(jnp.bfloat16)
        both[e, tokens, wide:] = over_last(g[i], pout[...]).astype(jnp.bfloat16)

    total = jnp.zeros((wide + narrow, wide + narrow), jnp.float32)
    for e in range(examples):
        sums = over_first(both[e], both[e])
        grads_ref[e] = sums[wide:, :wide]
        total = total + sums
    row = lax.broadcasted_iota(jnp.int32, (narrow, narrow), 0)
    col = lax.broadcasted_iota(jnp.int32, (narrow, narrow), 1)
    small = total[wide:, wide:]
    diagonal = jnp.sum(jnp.where(row == col, small, 0.0), axis=0, keepdims=True)
    spare = jnp.where(row == narrow - 1, diagonal, diagonal[:, narrow - 1 :])
    packed_ref[:narrow, :narrow] = jnp.where(col < row, small, total[:narrow, :narrow])
    packed_ref[:narrow, narrow:] = jnp.where(col < row, spare, total[narrow:wide, narrow:wide])
    packed_ref[narrow:, :narrow] = total[: narrow // 2, narrow:wide]
    packed_ref[narrow:, narrow:] = total[narrow // 2 : narrow, narrow:wide]


def project(x, g, pin, pout):
    examples, tokens, d = x.shape
    v = g.shape[2]
    wide, narrow = pin.shape[0], pout.shape[0]
    rows = divisor(tokens, 256)
    chunks = examples * (tokens // rows)
    return pl.pallas_call(
        project_kernel,
        out_shape=[
            pltpu.VMEM((narrow + narrow // 2, wide), jnp.float32),
            pltpu.VMEM((examples, narrow, wide), jnp.float32),
        ],
        in_specs=[pl.BlockSpec(memory_space=pl.ANY)] * 4,
        out_specs=[pl.BlockSpec(memory_space=VMEM)] * 2,
        scratch_shapes=[
            pltpu.VMEM((chunks, rows, d), x.dtype),
            pltpu.VMEM((chunks, rows, v), g.dtype),
            pltpu.VMEM((wide, d), pin.dtype),
            pltpu.VMEM((narrow, v), pout.dtype),
            pltpu.VMEM((d, wide), pin.dtype),
            pltpu.VMEM((examples, tokens, wide + narrow), jnp.bfloat16),
            pltpu.SemaphoreType.DMA((chunks,)),
            pltpu.SemaphoreType.DMA((chunks,)),
            pltpu.SemaphoreType.DMA((2,)),
        ],
        compiler_params=pltpu.CompilerParams(vmem_limit_bytes=60 * 2**20),
        name="project",
    )(x, g, pin, pout)


def factors(n):
    spread = n / (n + 2 * DAMP)
    result = []
    while spread > 2e-6:
        result.append(2 / (2 - spread * spread))
        spread = spread * spread / (2 - spread * spread)
    return result


def normalised(s):
    n = s.shape[0]
    eye = lax.broadcasted_iota(jnp.int32, (n, n), 0) == lax.broadcasted_iota(jnp.int32, (n, n), 1)
    diagonal = jnp.sum(jnp.where(eye, s, 0.0), axis=0, keepdims=True)
    mean = jnp.sum(diagonal, axis=1, keepdims=True) / n
    first = 2 / (n + 2 * DAMP)
    return (s / mean + jnp.where(eye, DAMP, 0.0)) * first, first / mean, eye


def score_rows(me, p_ref, e, tests, offsets, count):
    _, narrow, wide = p_ref.shape
    rows = tests.shape[0]
    per = rows // len(offsets)
    sums = jnp.zeros((rows, wide), jnp.float32)
    for o in range(narrow):
        sums = sums + tests[:, o * wide : (o + 1) * wide].astype(jnp.float32) * p_ref[e, o : o + 1, :]
    row = lax.broadcasted_iota(jnp.int32, (rows, 1), 0)
    target = jnp.zeros((rows, 1), jnp.int32)
    for i, offset in enumerate(offsets):
        inside = (row >= i * per) & (row < (i + 1) * per)
        target = jnp.where(inside, (me ^ offset) * per + row - i * per, target)
    lane = lax.broadcasted_iota(jnp.int32, (1, count), 1)
    by_row = jnp.sum(sums, axis=1, keepdims=True)
    return jnp.sum(jnp.where(target == lane, by_row, 0.0), axis=0, keepdims=True)


def precond_kernel(tokens, offsets, me_ref, packed_ref, grads_ref, tests_ref, out_ref, part_ref):
    wide = packed_ref.shape[1]
    examples, narrow, _ = grads_ref.shape
    packed = packed_ref[...]
    row = lax.broadcasted_iota(jnp.int32, (narrow, narrow), 0)
    col = lax.broadcasted_iota(jnp.int32, (narrow, narrow), 1)
    left, right = packed[:narrow, :narrow], packed[:narrow, narrow:]
    corner = jnp.concatenate([packed[narrow:, :narrow], packed[narrow:, narrow:]], axis=0)
    zero = jnp.zeros((narrow, narrow), jnp.float32)
    above = jnp.concatenate(
        [
            jnp.concatenate([jnp.where(col > row, left, 0.0), corner], axis=1),
            jnp.concatenate([zero, jnp.where(col > row, right, 0.0)], axis=1),
        ],
        axis=0,
    )
    middle = jnp.concatenate(
        [
            jnp.concatenate([jnp.where(col == row, left, 0.0), zero], axis=1),
            jnp.concatenate([zero, jnp.where(col == row, right, 0.0)], axis=1),
        ],
        axis=0,
    )
    yi, scale_in, _ = normalised(above + above.T + middle)
    below = jnp.where(col < row, left, 0.0)
    diagonal = jnp.where(col[:1] < narrow - 1, right[narrow - 1 :], right[narrow - 2 : narrow - 1, :1])
    yo, scale_out, eye = normalised(below + below.T + jnp.where(col == row, diagonal, 0.0))
    w = grads_ref[...].reshape(examples * narrow, wide)
    xo = jnp.where(eye, 1.0, 0.0)
    wides, narrows = factors(wide), factors(narrow)
    for k in range(max(len(wides), len(narrows))):
        times = exact if k < 5 else near_exact
        if k < len(wides):
            if k < len(wides) - 1:
                both = jnp.concatenate([yi, w], axis=0)
                both = wides[k] * (2 * both - times(both, yi))
                yi, w = both[:wide], both[wide:]
            else:
                w = wides[k] * (2 * w - times(w, yi))
        if k < len(narrows):
            if k < len(narrows) - 1:
                both = jnp.concatenate([yo, xo], axis=0)
                both = narrows[k] * (2 * both - times(both, yo))
                yo, xo = both[:narrow], both[narrow:]
            else:
                xo = narrows[k] * (2 * xo - times(xo, yo))
    scale = (scale_in * tokens) * (scale_out * tokens)
    for e in range(examples):
        both = near_exact(xo, w[e * narrow : (e + 1) * narrow]) * scale
        out_ref[e] = both.astype(jnp.bfloat16).astype(jnp.float32)
        part_ref[e : e + 1, :] = score_rows(me_ref[0], out_ref, e, tests_ref, offsets, part_ref.shape[1])


def precondition(me, packed, grads, tests, offsets, tokens, count):
    return pl.pallas_call(
        functools.partial(precond_kernel, float(tokens), offsets),
        out_shape=[pltpu.VMEM(grads.shape, jnp.float32), pltpu.VMEM((grads.shape[0], count), jnp.float32)],
        in_specs=[pl.BlockSpec(memory_space=SMEM)] + [pl.BlockSpec(memory_space=VMEM)] * 3,
        out_specs=[pl.BlockSpec(memory_space=VMEM)] * 2,
        compiler_params=pltpu.CompilerParams(vmem_limit_bytes=32 * 2**20),
        name="precondition",
    )(me, *[pltpu.with_memory_space_constraint(a, VMEM) for a in (packed, grads, tests)])


def score_kernel(sources, scale, me_ref, p_ref, part_ref, *refs):
    pieces, out_ref = refs[:-1], refs[-1]
    for e in range(p_ref.shape[0]):
        total = part_ref[e : e + 1, :]
        for t, offsets in zip(pieces, sources):
            total = total + score_rows(me_ref[0], p_ref, e, t, offsets, out_ref.shape[1])
        out_ref[e : e + 1, :] = total * scale


def score(me, precond, part, pieces, sources, scale):
    return pl.pallas_call(
        functools.partial(score_kernel, sources, scale),
        out_shape=jax.ShapeDtypeStruct(part.shape, jnp.float32),
        in_specs=[pl.BlockSpec(memory_space=SMEM)] + [pl.BlockSpec(memory_space=VMEM)] * (2 + len(pieces)),
        out_specs=pl.BlockSpec(memory_space=VMEM),
        compiler_params=pltpu.CompilerParams(vmem_limit_bytes=32 * 2**20),
        name="score",
    )(me, *[pltpu.with_memory_space_constraint(a, VMEM) for a in (precond, part, *pieces)])


def exchange(x, bit, devices):
    return lax.ppermute(x, "ex", [(i, i ^ bit) for i in range(devices)])


def join(tests, offsets, bit, devices):
    both = jnp.concatenate([tests, exchange(tests, bit, devices)], axis=0)
    return both, offsets + [k ^ bit for k in offsets]


def add_kernel(a_ref, b_ref, out_ref):
    out_ref[...] = a_ref[...] + b_ref[...]


def add_late(a, b, flops=LONG):
    return pl.pallas_call(
        add_kernel,
        out_shape=pltpu.VMEM(a.shape, a.dtype),
        in_specs=[pl.BlockSpec(memory_space=VMEM)] * 2,
        out_specs=pl.BlockSpec(memory_space=VMEM),
        cost_estimate=pl.CostEstimate(flops=flops, bytes_accessed=3 * a.size * 4, transcendentals=0),
        name="add",
    )(*[pltpu.with_memory_space_constraint(t, VMEM) for t in (a, b)])


def exchange_all(packed, tests, offsets, devices):
    far = devices // 4
    packed, tests = lax.optimization_barrier((packed, tests))
    packed = packed + exchange(packed, 1, devices)
    packed = packed + exchange(packed, 2, devices)
    while far > 4:
        tests, offsets = join(tests, offsets, far, devices)
        far //= 2
    packed, tests = lax.optimization_barrier((packed, tests))
    half, rows = len(offsets) // 2, tests.shape[0] // 2
    a, a_off = exchange(tests, 2, devices), [k ^ 2 for k in offsets]
    b, b_off = exchange(tests, 4, devices), [k ^ 4 for k in offsets]
    packed = add_late(packed, exchange(packed, 8, devices))
    bit = 16
    while bit < devices:
        packed = add_late(packed, exchange(packed, bit, devices), LONG // 5)
        bit *= 2
    c, c_off = exchange(b[:rows], 2, devices), [k ^ 2 for k in b_off[:half]]
    d, d_off = exchange(a[rows:], 4, devices), [k ^ 4 for k in a_off[half:]]
    packed = packed + exchange(packed, 4, devices)
    packed, c, d, tests, a, b = lax.optimization_barrier((packed, c, d, tests, a, b))
    everyone = jnp.concatenate([tests, a, b, c, d], axis=0)
    offsets = offsets + a_off + b_off + c_off + d_off
    pieces = [(everyone, offsets), (exchange(everyone, 1, devices), [k ^ 1 for k in offsets])]
    return packed, [t for t, _ in pieces], [off for _, off in pieces]


def on_device(example_inputs, output_grads, proj_in, proj_out, test_grads):
    examples, tokens, _ = example_inputs.shape
    wide, narrow = proj_in.shape[0], proj_out.shape[0]
    devices = lax.axis_size("ex")
    me = lax.axis_index("ex").astype(jnp.int32)
    simple = devices < 32 or devices & (devices - 1)
    if not simple:
        far = exchange(test_grads, devices // 2, devices)
    packed, grads = project(example_inputs, output_grads, proj_in, proj_out)
    if simple:
        packed = lax.psum(packed, "ex")
        pieces = [lax.all_gather(test_grads, "ex", axis=0, tiled=True)]
        sources = [list(range(devices))]
        me = me * 0
    else:
        packed, far = lax.optimization_barrier((packed, far))
        tests = jnp.concatenate([test_grads, far], axis=0)
        packed, pieces, sources = exchange_all(packed, tests, [0, devices // 2], devices)
    count = test_grads.shape[0] * devices
    precond, part = precondition(
        me[None], packed, grads, pieces[0], sources[0], examples * tokens * devices, count
    )
    scale = 4.0 / (wide * narrow * tokens) ** 0.5
    return score(me[None], precond, part, pieces[1:], sources[1:], scale)


def solution(mesh):
    return jax.shard_map(
        on_device,
        mesh=mesh,
        in_specs=(
            P(("grp", "ex"), None, None),
            P(("grp", "ex"), None, None),
            P(),
            P(),
            P("ex", None),
        ),
        out_specs=P(("grp", "ex"), None),
        check_vma=False,
    )
```

```python
import functools

import jax
import jax.numpy as jnp
from jax import lax
from jax.experimental import pallas as pl
from jax.experimental.pallas import tpu as pltpu
from jax.sharding import PartitionSpec as P

HIGHEST = lax.Precision.HIGHEST
DAMP = 0.1
DEPTH = 2
LONG = 10**10
VMEM = pltpu.MemorySpace.VMEM
SMEM = pltpu.MemorySpace.SMEM


def dot(a, b):
    return jnp.dot(a, b, preferred_element_type=jnp.float32)


def exact(a, b):
    return jnp.dot(a, b, precision=HIGHEST, preferred_element_type=jnp.float32)


def halves(a):
    high = a.astype(jnp.bfloat16)
    return high, (a - high.astype(jnp.float32)).astype(jnp.bfloat16)


def near_exact(a, b):
    (a_high, a_low), (b_high, b_low) = halves(a), halves(b)
    return dot(a_high, b_high) + (dot(a_low, b_high) + dot(a_high, b_low))


def over_last(a, b):
    return lax.dot_general(a, b, (((1,), (1,)), ((), ())), preferred_element_type=jnp.float32)


def over_first(a, b):
    return lax.dot_general(a, b, (((0,), (0,)), ((), ())), preferred_element_type=jnp.float32)


def divisor(n, most):
    return max(d for d in range(1, most + 1) if n % d == 0)


def project_kernel(x_hbm, g_hbm, pin_hbm, pout_hbm, packed_ref, grads_ref, x, g, pin, pout, pin_t, both, sx, sg, sp):
    examples = x_hbm.shape[0]
    wide, narrow = pin.shape[0], pout.shape[0]
    chunks, rows = x.shape[:2]
    per = chunks // examples
    pin_copy = pltpu.make_async_copy(pin_hbm, pin, sp.at[0])
    pout_copy = pltpu.make_async_copy(pout_hbm, pout, sp.at[1])
    pin_copy.start()
    pout_copy.start()

    def place(i):
        return i // per, pl.ds((i % per) * rows, rows)

    def copies(i):
        return (
            pltpu.make_async_copy(x_hbm.at[place(i)], x.at[i], sx.at[i]),
            pltpu.make_async_copy(g_hbm.at[place(i)], g.at[i], sg.at[i]),
        )

    for i in range(min(DEPTH, chunks)):
        for copy in copies(i):
            copy.start()
    pin_copy.wait()
    if DEPTH < chunks:
        for copy in copies(DEPTH):
            copy.start()
    pin_t[...] = pin[...].T
    pout_copy.wait()

    for i in range(chunks):
        for copy in copies(i):
            copy.wait()

        if i + DEPTH + 1 < chunks:
            for copy in copies(i + DEPTH + 1):
                copy.start()

        e, tokens = place(i)
        both[e, tokens, :wide] = dot(x[i], pin_t[...]).astype(jnp.bfloat16)
        both[e, tokens, wide:] = over_last(g[i], pout[...]).astype(jnp.bfloat16)

    total = jnp.zeros((wide + narrow, wide + narrow), jnp.float32)
    for e in range(examples):
        sums = over_first(both[e], both[e])
        grads_ref[e] = sums[wide:, :wide]
        total = total + sums
    row = lax.broadcasted_iota(jnp.int32, (narrow, narrow), 0)
    col = lax.broadcasted_iota(jnp.int32, (narrow, narrow), 1)
    small = total[wide:, wide:]
    diagonal = jnp.sum(jnp.where(row == col, small, 0.0), axis=0, keepdims=True)
    spare = jnp.where(row == narrow - 1, diagonal, diagonal[:, narrow - 1 :])
    packed_ref[:narrow, :narrow] = jnp.where(col < row, small, total[:narrow, :narrow])
    packed_ref[:narrow, narrow:] = jnp.where(col < row, spare, total[narrow:wide, narrow:wide])
    packed_ref[narrow:, :narrow] = total[: narrow // 2, narrow:wide]
    packed_ref[narrow:, narrow:] = total[narrow // 2 : narrow, narrow:wide]


def project(x, g, pin, pout):
    examples, tokens, d = x.shape
    v = g.shape[2]
    wide, narrow = pin.shape[0], pout.shape[0]
    rows = divisor(tokens, 256)
    chunks = examples * (tokens // rows)
    return pl.pallas_call(
        project_kernel,
        out_shape=[
            pltpu.VMEM((narrow + narrow // 2, wide), jnp.float32),
            pltpu.VMEM((examples, narrow, wide), jnp.float32),
        ],
        in_specs=[pl.BlockSpec(memory_space=pl.ANY)] * 4,
        out_specs=[pl.BlockSpec(memory_space=VMEM)] * 2,
        scratch_shapes=[
            pltpu.VMEM((chunks, rows, d), x.dtype),
            pltpu.VMEM((chunks, rows, v), g.dtype),
            pltpu.VMEM((wide, d), pin.dtype),
            pltpu.VMEM((narrow, v), pout.dtype),
            pltpu.VMEM((d, wide), pin.dtype),
            pltpu.VMEM((examples, tokens, wide + narrow), jnp.bfloat16),
            pltpu.SemaphoreType.DMA((chunks,)),
            pltpu.SemaphoreType.DMA((chunks,)),
            pltpu.SemaphoreType.DMA((2,)),
        ],
        compiler_params=pltpu.CompilerParams(vmem_limit_bytes=60 * 2**20),
        name="project",
    )(x, g, pin, pout)


def factors(n):
    spread = n / (n + 2 * DAMP)
    result = []
    while spread > 2e-6:
        result.append(2 / (2 - spread * spread))
        spread = spread * spread / (2 - spread * spread)
    return result


def normalised(s):
    n = s.shape[0]
    eye = lax.broadcasted_iota(jnp.int32, (n, n), 0) == lax.broadcasted_iota(jnp.int32, (n, n), 1)
    diagonal = jnp.sum(jnp.where(eye, s, 0.0), axis=0, keepdims=True)
    mean = jnp.sum(diagonal, axis=1, keepdims=True) / n
    first = 2 / (n + 2 * DAMP)
    return (s / mean + jnp.where(eye, DAMP, 0.0)) * first, first / mean, eye


def score_rows(me, p_ref, e, tests, offsets, count):
    _, narrow, wide = p_ref.shape
    rows = tests.shape[0]
    per = rows // len(offsets)
    sums = jnp.zeros((rows, wide), jnp.float32)
    for o in range(narrow):
        sums = sums + tests[:, o * wide : (o + 1) * wide].astype(jnp.float32) * p_ref[e, o : o + 1, :]
    row = lax.broadcasted_iota(jnp.int32, (rows, 1), 0)
    target = jnp.zeros((rows, 1), jnp.int32)
    for i, offset in enumerate(offsets):
        inside = (row >= i * per) & (row < (i + 1) * per)
        target = jnp.where(inside, (me ^ offset) * per + row - i * per, target)
    lane = lax.broadcasted_iota(jnp.int32, (1, count), 1)
    by_row = jnp.sum(sums, axis=1, keepdims=True)
    return jnp.sum(jnp.where(target == lane, by_row, 0.0), axis=0, keepdims=True)


def precond_kernel(tokens, offsets, me_ref, packed_ref, grads_ref, tests_ref, out_ref, part_ref):
    wide = packed_ref.shape[1]
    examples, narrow, _ = grads_ref.shape
    packed = packed_ref[...]
    row = lax.broadcasted_iota(jnp.int32, (narrow, narrow), 0)
    col = lax.broadcasted_iota(jnp.int32, (narrow, narrow), 1)
    left, right = packed[:narrow, :narrow], packed[:narrow, narrow:]
    corner = jnp.concatenate([packed[narrow:, :narrow], packed[narrow:, narrow:]], axis=0)
    zero = jnp.zeros((narrow, narrow), jnp.float32)
    above = jnp.concatenate(
        [
            jnp.concatenate([jnp.where(col > row, left, 0.0), corner], axis=1),
            jnp.concatenate([zero, jnp.where(col > row, right, 0.0)], axis=1),
        ],
        axis=0,
    )
    middle = jnp.concatenate(
        [
            jnp.concatenate([jnp.where(col == row, left, 0.0), zero], axis=1),
            jnp.concatenate([zero, jnp.where(col == row, right, 0.0)], axis=1),
        ],
        axis=0,
    )
    yi, scale_in, _ = normalised(above + above.T + middle)
    below = jnp.where(col < row, left, 0.0)
    diagonal = jnp.where(col[:1] < narrow - 1, right[narrow - 1 :], right[narrow - 2 : narrow - 1, :1])
    yo, scale_out, eye = normalised(below + below.T + jnp.where(col == row, diagonal, 0.0))
    w = grads_ref[...].reshape(examples * narrow, wide)
    xo = jnp.where(eye, 1.0, 0.0)
    wides, narrows = factors(wide), factors(narrow)
    for k in range(max(len(wides), len(narrows))):
        times = exact if k < 4 else near_exact
        if k < len(wides):
            if k < len(wides) - 1:
                both = jnp.concatenate([yi, w], axis=0)
                both = wides[k] * (2 * both - times(both, yi))
                yi, w = both[:wide], both[wide:]
            else:
                w = wides[k] * (2 * w - times(w, yi))
        if k < len(narrows):
            if k < len(narrows) - 1:
                both = jnp.concatenate([yo, xo], axis=0)
                both = narrows[k] * (2 * both - times(both, yo))
                yo, xo = both[:narrow], both[narrow:]
            else:
                xo = narrows[k] * (2 * xo - times(xo, yo))
    scale = (scale_in * tokens) * (scale_out * tokens)
    for e in range(examples):
        both = near_exact(xo, w[e * narrow : (e + 1) * narrow]) * scale
        out_ref[e] = both.astype(jnp.bfloat16).astype(jnp.float32)
        part_ref[e : e + 1, :] = score_rows(me_ref[0], out_ref, e, tests_ref, offsets, part_ref.shape[1])


def precondition(me, packed, grads, tests, offsets, tokens, count):
    return pl.pallas_call(
        functools.partial(precond_kernel, float(tokens), offsets),
        out_shape=[pltpu.VMEM(grads.shape, jnp.float32), pltpu.VMEM((grads.shape[0], count), jnp.float32)],
        in_specs=[pl.BlockSpec(memory_space=SMEM)] + [pl.BlockSpec(memory_space=VMEM)] * 3,
        out_specs=[pl.BlockSpec(memory_space=VMEM)] * 2,
        compiler_params=pltpu.CompilerParams(vmem_limit_bytes=32 * 2**20),
        name="precondition",
    )(me, *[pltpu.with_memory_space_constraint(a, VMEM) for a in (packed, grads, tests)])


def score_kernel(sources, scale, me_ref, p_ref, part_ref, *refs):
    pieces, out_ref = refs[:-1], refs[-1]
    for e in range(p_ref.shape[0]):
        total = part_ref[e : e + 1, :]
        for t, offsets in zip(pieces, sources):
            total = total + score_rows(me_ref[0], p_ref, e, t, offsets, out_ref.shape[1])
        out_ref[e : e + 1, :] = total * scale


def score(me, precond, part, pieces, sources, scale):
    return pl.pallas_call(
        functools.partial(score_kernel, sources, scale),
        out_shape=jax.ShapeDtypeStruct(part.shape, jnp.float32),
        in_specs=[pl.BlockSpec(memory_space=SMEM)] + [pl.BlockSpec(memory_space=VMEM)] * (2 + len(pieces)),
        out_specs=pl.BlockSpec(memory_space=VMEM),
        compiler_params=pltpu.CompilerParams(vmem_limit_bytes=32 * 2**20),
        name="score",
    )(me, *[pltpu.with_memory_space_constraint(a, VMEM) for a in (precond, part, *pieces)])


def exchange(x, bit, devices):
    return lax.ppermute(x, "ex", [(i, i ^ bit) for i in range(devices)])


def join(tests, offsets, bit, devices):
    both = jnp.concatenate([tests, exchange(tests, bit, devices)], axis=0)
    return both, offsets + [k ^ bit for k in offsets]


def add_kernel(a_ref, b_ref, out_ref):
    out_ref[...] = a_ref[...] + b_ref[...]


def add_late(a, b, flops=LONG):
    return pl.pallas_call(
        add_kernel,
        out_shape=pltpu.VMEM(a.shape, a.dtype),
        in_specs=[pl.BlockSpec(memory_space=VMEM)] * 2,
        out_specs=pl.BlockSpec(memory_space=VMEM),
        cost_estimate=pl.CostEstimate(flops=flops, bytes_accessed=3 * a.size * 4, transcendentals=0),
        name="add",
    )(*[pltpu.with_memory_space_constraint(t, VMEM) for t in (a, b)])


def exchange_all(packed, tests, offsets, devices):
    far = devices // 4
    packed, tests = lax.optimization_barrier((packed, tests))
    packed = packed + exchange(packed, 1, devices)
    packed = packed + exchange(packed, 2, devices)
    while far > 4:
        tests, offsets = join(tests, offsets, far, devices)
        far //= 2
    packed, tests = lax.optimization_barrier((packed, tests))
    half, rows = len(offsets) // 2, tests.shape[0] // 2
    a, a_off = exchange(tests, 2, devices), [k ^ 2 for k in offsets]
    b, b_off = exchange(tests, 4, devices), [k ^ 4 for k in offsets]
    packed = add_late(packed, exchange(packed, 8, devices))
    bit = 16
    while bit < devices:
        packed = add_late(packed, exchange(packed, bit, devices), LONG // 5)
        bit *= 2
    c, c_off = exchange(b[:rows], 2, devices), [k ^ 2 for k in b_off[:half]]
    d, d_off = exchange(a[rows:], 4, devices), [k ^ 4 for k in a_off[half:]]
    packed = packed + exchange(packed, 4, devices)
    packed, c, d, tests, a, b = lax.optimization_barrier((packed, c, d, tests, a, b))
    everyone = jnp.concatenate([tests, a, b, c, d], axis=0)
    offsets = offsets + a_off + b_off + c_off + d_off
    pieces = [(everyone, offsets), (exchange(everyone, 1, devices), [k ^ 1 for k in offsets])]
    return packed, [t for t, _ in pieces], [off for _, off in pieces]


def on_device(example_inputs, output_grads, proj_in, proj_out, test_grads):
    examples, tokens, _ = example_inputs.shape
    wide, narrow = proj_in.shape[0], proj_out.shape[0]
    devices = lax.axis_size("ex")
    me = lax.axis_index("ex").astype(jnp.int32)
    simple = devices < 32 or devices & (devices - 1)
    if not simple:
        far = exchange(test_grads, devices // 2, devices)
    packed, grads = project(example_inputs, output_grads, proj_in, proj_out)
    if simple:
        packed = lax.psum(packed, "ex")
        pieces = [lax.all_gather(test_grads, "ex", axis=0, tiled=True)]
        sources = [list(range(devices))]
        me = me * 0
    else:
        packed, far = lax.optimization_barrier((packed, far))
        tests = jnp.concatenate([test_grads, far], axis=0)
        packed, pieces, sources = exchange_all(packed, tests, [0, devices // 2], devices)
    count = test_grads.shape[0] * devices
    precond, part = precondition(
        me[None], packed, grads, pieces[0], sources[0], examples * tokens * devices, count
    )
    scale = 4.0 / (wide * narrow * tokens) ** 0.5
    return score(me[None], precond, part, pieces[1:], sources[1:], scale)


def solution(mesh):
    return jax.shard_map(
        on_device,
        mesh=mesh,
        in_specs=(
            P(("grp", "ex"), None, None),
            P(("grp", "ex"), None, None),
            P(),
            P(),
            P("ex", None),
        ),
        out_specs=P(("grp", "ex"), None),
        check_vma=False,
    )
```
